512 devices in a mesh: member: 32 (over z_lo, x), tile: 16 (over z_hi, y, core).
Axes of the slice: x: 4, y: 4, z: 16 (z_hi: 2, z_lo: 8; z = z_hi * 8 + z_lo), core: 2. Of those that a mesh axis runs over, the one named last changes fastest.
Arguments:
- increment: bfloat16 [32, 64, 32, 1280], P('member', None, 'tile'), may hold values from -6 to 6
- courant_x: bfloat16 [64, 32, 1280], P(None, 'tile'), may hold values from 0.049804688 to 0.34960938
- courant_y: bfloat16 [64, 32, 1280], P(None, 'tile'), may hold values from 0.049804688 to 0.34960938
- diffusivity: float32 [64], replicated, may hold values from 0.01 to 0.07
- column_inverse: float32 [64, 64, 64], P('tile')
- jacobian: float32 [256, 64], replicated, may hold values from -0.75 to 0.75
- obs_cells: int32 [4, 4096], P(None, 'tile'), may hold values from 0 to 40959, as said below
- owner: int32 [4], replicated, may hold values from 0 to 31
- channel_mask: int32 [4, 256], replicated, may hold values 0 or 1
- departures: bfloat16 [32, 4, 256, 4096], P('member', None, None, 'tile'), may hold values from -6 to 6
Outputs:
- final_state: bfloat16 [32, 64, 32, 1280], P('member', None, 'tile')
- innovations: float32 [32, 4, 256, 4096], P('member', None, None, 'tile')
- perturbed: bfloat16 [32, 4, 256, 4096], P('member', None, None, 'tile')
The draws below stay inside these ranges and needn't reach their ends.
Inputs may be any that keep to these rules, and one draw needn't show every extreme that they name: `obs_cells`: entry o of each slot names a cell in latitude rows 2 * (o // 256) to 2 * (o // 256) + 1, cells numbered row-major over the 32 x 1280 grid.
All inputs are finite; a program needn't handle non-finite values.
Results may differ from the reference program's by a relative error of at most 0.009.
Values may be sent and summed in bfloat16 or wider, within the bound.
No kernel may reach another device: no remote copies, remote signals or barrier semaphores. Data moves between devices by JAX's collectives and lax.ppermute only.
A program may use at most 64 MiB of HBM per device.

```python
import math
import jax
import jax.numpy as jnp
from jax import lax

LEV = 64
CH = 256
SLOTS = 4
ROWS_DEV = 2
OBS_DEV = 256
MEMBERS = 32
NY = 32
NX = 1280
NBLK = 64
NOBS = 4096


def draw_column_inverse(key, part):
    key = jax.random.fold_in(key, 11)
    first, second = jax.random.split(key)
    diagonal = jax.random.uniform(first, (NBLK, LEV), jnp.float32, 0.5, 0.7)
    spread = jax.random.normal(second, (NBLK, LEV, LEV), jnp.float32) * (0.24 / LEV ** 0.5)
    identity = jnp.eye(LEV, dtype=jnp.float32)
    return spread + diagonal[:, :, None] * identity[None]


def draw_obs_cells(key, part):
    key = jax.random.fold_in(key, 12)
    local = jax.random.randint(key, (SLOTS, NOBS), 0, ROWS_DEV * NX, dtype=jnp.int32)
    local = local.at[0, 0].set(0)
    local = local.at[0, NOBS - 1].set(ROWS_DEV * NX - 1)
    band = jnp.arange(NOBS, dtype=jnp.int32) // OBS_DEV * (ROWS_DEV * NX)
    return local + band[None, :]


def touch_ends(array, stream_key, smallest, largest):
    spot = [jax.random.randint(jax.random.fold_in(stream_key, axis), (), 0, length) for axis, length in enumerate(array.shape)]
    widest = array.shape.index(max(array.shape))
    next_to = spot[:widest] + [(spot[widest] + 1) % array.shape[widest]] + spot[widest + 1:]
    return array.at[tuple(spot)].set(smallest).at[tuple(next_to)].set(largest)


def shard_levels(stream_key, shape, cuts, smallest, high):
    def one(axis_at, blocks):
        draws = jax.random.uniform(jax.random.fold_in(jax.random.fold_in(stream_key, 6), axis_at), (blocks,), jnp.float32, smallest / len(cuts), high / len(cuts))
        return jnp.repeat(jnp.exp(draws), shape[axis_at] // blocks).reshape((-1,) + (1,) * (len(shape) - axis_at - 1))

    factor_of = one(*cuts[0])
    for cut in cuts[1:]:
        factor_of = factor_of * one(*cut)
    return factor_of


def gaussian(stream_key, extent, width, limit, cuts=(), kind=jnp.bfloat16):
    array = width * jax.random.normal(stream_key, extent, jnp.float32)
    if cuts:
        array = array * shard_levels(stream_key, extent, cuts, -0.22, 0.18)
    return jnp.clip(array, -limit, limit).astype(kind)


def setup_inputs(seed: int = 0) -> dict:
    keys = jax.random.split(jax.random.key(seed), 11)
    increment = gaussian(keys[0], (MEMBERS, LEV, NY, NX), 1.0, 6.0, ((0, 32), (2, 16)))
    courant_x = jnp.clip(0.049804688 + 0.2998047 * jax.random.uniform(keys[1], (LEV, NY, NX), jnp.float32) ** shard_levels(keys[1], (LEV, NY, NX), ((1, 16),), -0.2, 0.2), 0.049804688, 0.34960938).astype(jnp.bfloat16)
    courant_y = jnp.clip(0.049804688 + 0.2998047 * jax.random.uniform(keys[2], (LEV, NY, NX), jnp.float32) ** shard_levels(keys[2], (LEV, NY, NX), ((1, 16),), -0.2, 0.2), 0.049804688, 0.34960938).astype(jnp.bfloat16)
    diffusivity = jnp.clip(jnp.exp(jax.random.uniform(keys[3], (LEV,), jnp.float32, math.log(0.01), math.log(0.07))), 0.01, 0.07)
    column_inverse = draw_column_inverse(jax.random.fold_in(keys[10], 71), 0)
    jacobian = gaussian(keys[5], (CH, LEV), LEV ** -0.5, 0.75, (), jnp.float32)
    obs_cells = draw_obs_cells(jax.random.fold_in(keys[10], 71), 0)
    owner = touch_ends(jax.random.randint(keys[7], (SLOTS,), 0, MEMBERS), jax.random.fold_in(keys[7], 1), 0, MEMBERS - 1).astype(jnp.int32)
    channel_mask = touch_ends((jax.random.randint(keys[8], (SLOTS, CH), 0, 4) < 3).astype(jnp.int32), jax.random.fold_in(keys[8], 1), 0, 1)
    departures = gaussian(keys[9], (MEMBERS, SLOTS, CH, NOBS), 1.0, 6.0, ((0, 32), (3, 16)))
    return dict(increment=increment, courant_x=courant_x, courant_y=courant_y, diffusivity=diffusivity, column_inverse=column_inverse, jacobian=jacobian, obs_cells=obs_cells, owner=owner, channel_mask=channel_mask, departures=departures)


def advance(state_field, padded, courant_east, courant_north, diffusivity):
    southern = padded[:, :-2]
    northern = padded[:, 2:]
    western = jnp.roll(state_field, 1, axis=2)
    eastern = jnp.roll(state_field, -1, axis=2)
    spread = diffusivity[:, None, None] * (eastern + western + northern + southern - 4.0 * state_field)
    return state_field - courant_east * (state_field - western) - courant_north * (state_field - southern) + spread


def vertical(state_field, inverse):
    level_count, row_count, lon_count = state_field.shape
    block_count = inverse.shape[0]
    grouped = state_field.reshape(level_count, row_count, block_count, lon_count // block_count)
    mixed = jnp.einsum('bkl,lybw->kybw', inverse, grouped, precision=lax.Precision.HIGHEST)
    return mixed.reshape(level_count, row_count, lon_count)


def reference(increment, courant_x, courant_y, diffusivity, column_inverse, jacobian, obs_cells, owner, channel_mask, departures):
    courant_east = courant_x.astype(jnp.float32)
    courant_north = courant_y.astype(jnp.float32)

    def member_run(initial):
        state_field = initial.astype(jnp.float32)
        modeled_list = []
        for slot_index in range(SLOTS):
            padded = jnp.pad(state_field, ((0, 0), (1, 1), (0, 0)))
            state_field = advance(state_field, padded, courant_east, courant_north, diffusivity)
            state_field = vertical(state_field, column_inverse)
            columns_all = state_field.reshape(LEV, NY * NX)
            picked = jnp.take(columns_all, obs_cells[slot_index], axis=1)
            modeled_list.append(jnp.dot(jacobian, picked, precision=lax.Precision.HIGHEST))
        return state_field.astype(jnp.bfloat16), jnp.stack(modeled_list)

    states, modeled = lax.map(member_run, increment)
    ensemble_mean = jnp.sum(modeled, axis=0) / MEMBERS
    owned = departures[owner, jnp.arange(SLOTS, dtype=jnp.int32)].astype(jnp.float32)
    innovations = jnp.where(channel_mask[None, :, :, None] == 1, owned[None] - modeled, jnp.float32(0.0))
    perturbed = (modeled - ensemble_mean[None]).astype(jnp.bfloat16)
    return states, innovations, perturbed
```

```python
import functools

import jax
import jax.numpy as jnp
from jax import lax
from jax.experimental import pallas as pl
from jax.experimental.pallas import tpu as pltpu
from jax.sharding import PartitionSpec as P

F32 = jnp.float32
BF16 = jnp.bfloat16
SLOTS = 4
LEV = 64
NX = 1280
WIDE = 20
LANES = 128
TILES = NX // LANES
OBS = 256
CH = 256
VMEM = pl.BlockSpec(memory_space=pltpu.VMEM)
SMEM = pl.BlockSpec(memory_space=pltpu.SMEM)


def split(value):
    high = value.astype(BF16)
    return high, (value - high.astype(F32)).astype(BF16)


def stacked(value):
    high, low = split(value)
    return jnp.concatenate([high, high, low, low], axis=0)


def horizontal(centre, south, north, east_number, north_number, spread):
    west = pltpu.roll(centre, 1, 1)
    east = pltpu.roll(centre, NX - 1, 1)
    return (
        centre
        - east_number * (centre - west)
        - north_number * (centre - south)
        + spread * (east + west + north + south - 4.0 * centre)
    )


def vertical(matrices, high, low, rows, store):
    width = len(rows) * LANES
    lane = lax.broadcasted_iota(jnp.int32, (LEV, width), 1) % LANES
    for tile in range(TILES):
        cut = slice(tile * LANES, (tile + 1) * LANES)
        upper = jnp.concatenate([high[row, :, cut] for row in rows], axis=1)
        lower = jnp.concatenate([low[row, :, cut] for row in rows], axis=1)
        right = jnp.concatenate([upper, upper, lower, lower], axis=0)
        first = tile * LANES // WIDE
        last = (tile * LANES + LANES - 1) // WIDE
        left = matrices[first * LEV : (last + 1) * LEV, :]
        left = jnp.concatenate([left, left], axis=1)
        mixed = jnp.dot(left, right, preferred_element_type=F32)
        out = mixed[:LEV]
        for block in range(first + 1, last + 1):
            at = (block - first) * LEV
            out = jnp.where(lane >= block * WIDE - tile * LANES, mixed[at : at + LEV], out)
        for place, row in enumerate(rows):
            store(row, cut, out[:, place * LANES : (place + 1) * LANES])


def pick(read, cells, out_ref, at):
    total = jnp.zeros((2 * LEV, OBS), F32)
    steps = NX // 256
    for chunk in range(2 * steps):
        row, start = chunk // steps, (chunk % steps) * 256
        left = jnp.concatenate(split(read(row, slice(start, start + 256))), axis=0)
        cell = lax.broadcasted_iota(jnp.int32, (256, OBS), 0) + chunk * 256
        chosen = jnp.where(cell == cells, 1.0, 0.0).astype(BF16)
        total = total + jnp.dot(left, chosen, preferred_element_type=F32)
    value = total[:LEV] + total[LEV:]
    out_ref[at : at + LEV, :] = value[:, :LANES]
    out_ref[at + LEV : at + 2 * LEV, :] = value[:, LANES:]


def first_kernel(
    place, own, south, north, spread_ref, near, far, cells,
    state_out, halo_out, picked_out, matrices_out,
    state, high, low,
):
    here = place[0]
    for core in range(2):
        piece = near if core == 0 else far
        for y in range(4):
            for z in range(2):
                tile = jnp.bitwise_xor(here & 9, 8 * z + core) + 2 * y
                at = pl.multiple_of(tile * 256, 256)
                matrices_out[pl.ds(at, 256), :] = piece[y, z * 256 : (z + 1) * 256, :]
    spread = spread_ref[...]
    low_keep = jnp.where(here == 0, 0.0, 1.0)
    high_keep = jnp.where(here == 15, 0.0, 1.0)
    line = [south[0], south[1], own[2], own[3], north[2], north[3]]
    east_of = [south[2], own[0], own[4], north[0]]
    north_of = [south[3], own[1], own[5], north[1]]
    line = [value.astype(F32) for value in line]
    for row in range(4):
        value = horizontal(
            line[row + 1], line[row], line[row + 2],
            east_of[row].astype(F32), north_of[row].astype(F32), spread,
        )
        if row == 0:
            value = value * low_keep
        if row == 3:
            value = value * high_keep
        high[row], low[row] = split(value)

    def keep(row, cut, value):
        state[row, :, cut] = value

    vertical(matrices_out, high, low, range(4), keep)
    pick(lambda row, cut: state[row + 1, :, cut], cells[0:1, :], picked_out, 0)
    for row in range(2):
        value = horizontal(
            state[row + 1], state[row], state[row + 2],
            east_of[row + 1].astype(F32), north_of[row + 1].astype(F32), spread,
        )
        high[row], low[row] = split(value)

    def give(row, cut, value):
        state_out[row, :, cut] = value
        halo_out[row, :, cut] = value.astype(BF16)

    vertical(matrices_out, high, low, range(2), give)
    pick(lambda row, cut: state_out[row, :, cut], cells[1:2, :], picked_out, 2 * LEV)


def second_kernel(
    place, own, south_of, north_of_tile, mid, south, north, spread_ref, matrices, cells,
    final_out, picked_out,
    state, high, low,
):
    here = place[0]
    spread = spread_ref[...]
    low_keep = jnp.where(here == 0, 0.0, 1.0)
    high_keep = jnp.where(here == 15, 0.0, 1.0)
    line = [south[0].astype(F32), south[1].astype(F32), mid[0], mid[1], north[0].astype(F32), north[1].astype(F32)]
    east_of = [south_of[2], own[0], own[4], north_of_tile[0]]
    north_of = [south_of[3], own[1], own[5], north_of_tile[1]]
    for row in range(4):
        value = horizontal(
            line[row + 1], line[row], line[row + 2],
            east_of[row].astype(F32), north_of[row].astype(F32), spread,
        )
        if row == 0:
            value = value * low_keep
        if row == 3:
            value = value * high_keep
        high[row], low[row] = split(value)

    def keep(row, cut, value):
        state[row, :, cut] = value

    vertical(matrices, high, low, range(4), keep)
    pick(lambda row, cut: state[row + 1, :, cut], cells[2:3, :], picked_out, 0)
    for row in range(2):
        value = horizontal(
            state[row + 1], state[row], state[row + 2],
            east_of[row + 1].astype(F32), north_of[row + 1].astype(F32), spread,
        )
        high[row], low[row] = split(value)

    def give(row, cut, value):
        state[row, :, cut] = value
        final_out[row, :, cut] = value.astype(BF16)

    vertical(matrices, high, low, range(2), give)
    pick(lambda row, cut: state[row, :, cut], cells[3:4, :], picked_out, 2 * LEV)


def operator(jacobian_ref):
    high, low = split(jacobian_ref[...])
    return jnp.concatenate([high, low, high, low], axis=1)


def innovations_kernel(jacobian_ref, early, late, owned, mask, out_ref):
    left = operator(jacobian_ref)
    for slot in range(SLOTS):
        picked = early if slot < 2 else late
        at = (slot % 2) * 2 * LEV
        right = jnp.concatenate([picked[at : at + LEV, :], picked[at + LEV : at + 2 * LEV, :]], axis=1)
        modeled = jnp.dot(left, stacked(right), preferred_element_type=F32)
        used = mask[:, slot : slot + 1] == 1
        out_ref[slot] = jnp.where(used, owned[slot].astype(F32) - modeled, 0.0)


def perturbed_kernel(jacobian_ref, early, late, mean, out_ref):
    left = operator(jacobian_ref)
    for slot in range(SLOTS):
        picked = early if slot < 2 else late
        at = (slot % 2) * 2 * LEV
        whole = slot * 2 * LEV
        right = jnp.concatenate(
            [
                picked[at + half : at + half + LEV, :] - mean[whole + half : whole + half + LEV, :].astype(F32)
                for half in (0, LEV)
            ],
            axis=1,
        )
        out_ref[slot] = jnp.dot(left, stacked(right), preferred_element_type=F32).astype(BF16)


def call(kernel, out_shape, in_specs, scratch=(), flops=0, traffic=0):
    return pl.pallas_call(
        kernel,
        out_shape=out_shape,
        in_specs=in_specs,
        out_specs=jax.tree.map(lambda _: VMEM, out_shape),
        scratch_shapes=list(scratch),
        compiler_params=pltpu.CompilerParams(vmem_limit_bytes=40 * 1024 * 1024),
        cost_estimate=pl.CostEstimate(flops=flops, bytes_accessed=traffic, transcendentals=0),
    )


def shape(*sizes, dtype=F32):
    return jax.ShapeDtypeStruct(sizes, dtype)


def gathered_from(value, axis, groups):
    count = len(groups[0])
    copies = jnp.broadcast_to(value[None], (count, *value.shape))
    return lax.all_to_all(copies, axis, 0, 0, tiled=True, axis_index_groups=groups)


def local(
    increment,
    courant_x,
    courant_y,
    diffusivity,
    column_inverse,
    jacobian,
    obs_cells,
    owner,
    channel_mask,
    departures,
):
    here = lax.axis_index("tile")
    member = lax.axis_index("member")
    place = jnp.reshape(here, (1,)).astype(jnp.int32)

    inverse = column_inverse.reshape(4 * LEV, LEV)
    upper = lax.reduce_precision(inverse, exponent_bits=8, mantissa_bits=7)
    halves = jnp.concatenate([upper.astype(BF16), (inverse - upper).astype(BF16)], axis=1)
    mirrored = [
        ((z * 4 + x) * 16 + tile, ((7 - z) * 4 + x) * 16 + (tile ^ 8))
        for z in range(8)
        for x in range(4)
        for tile in range(16)
    ]
    other = lax.ppermute(halves, ("member", "tile"), mirrored)
    pair = jnp.concatenate([halves, other], axis=0)
    y_groups = [[8 * z + 2 * y + core for y in range(4)] for z in range(2) for core in range(2)]
    near = gathered_from(pair, "tile", y_groups).reshape(4, 512, LANES)
    far = lax.ppermute(near, "tile", [(i, i ^ 1) for i in range(16)])

    rows_in = jnp.swapaxes(increment[0], 0, 1)
    x_rows = jnp.swapaxes(courant_x, 0, 1)
    y_rows = jnp.swapaxes(courant_y, 0, 1)
    own = jnp.concatenate([x_rows[:1], y_rows[:1], rows_in, x_rows[1:], y_rows[1:]], axis=0)
    forward = [(i, i + 1) for i in range(15)]
    backward = [(i + 1, i) for i in range(15)]
    south = lax.ppermute(own[2:], "tile", forward)
    north = lax.ppermute(own[:4], "tile", backward)

    order = [[(p % 8) * 4 + p // 8 for p in range(32)]]
    pieces = lax.all_to_all(
        departures.reshape(32, 32, OBS), "member", 0, 0, tiled=True, axis_index_groups=order
    ).reshape(32, 32, OBS)
    slot_owner = lax.dynamic_index_in_dim(owner, member % 4, keepdims=False)
    source = (slot_owner % 4) * 8 + slot_owner // 4
    kept = lax.dynamic_index_in_dim(pieces, source, keepdims=False)
    owned = gathered_from(kept, "member", order).reshape(SLOTS, CH, OBS)

    cells = obs_cells - here * (2 * NX)
    spread = jnp.broadcast_to(diffusivity[:, None], (LEV, NX))
    window = [
        pltpu.VMEM((4, LEV, NX), F32),
        pltpu.VMEM((4, LEV, NX), BF16),
        pltpu.VMEM((4, LEV, NX), BF16),
    ]
    mid, halo, early, matrices = call(
        first_kernel,
        (
            shape(2, LEV, NX),
            shape(2, LEV, NX, dtype=BF16),
            shape(4 * LEV, LANES),
            shape(64 * LEV, LANES, dtype=BF16),
        ),
        [SMEM] + [VMEM] * 7,
        window,
        flops=2_000_000_000,
        traffic=8_000_000,
    )(place, own, south, north, spread, near, far, cells)
    south_mid = lax.ppermute(halo, "tile", forward)
    north_mid = lax.ppermute(halo, "tile", backward)
    final, late = call(
        second_kernel,
        (shape(2, LEV, NX, dtype=BF16), shape(4 * LEV, LANES)),
        [SMEM] + [VMEM] * 9,
        window,
        flops=2_000_000_000,
        traffic=8_000_000,
    )(place, own, south, north, mid, south_mid, north_mid, spread, matrices, cells)

    both = jnp.concatenate([early, late], axis=0).astype(BF16).reshape(32, 16, LANES)
    members = [list(range(32))]
    parts = lax.all_to_all(both, "member", 0, 0, tiled=True, axis_index_groups=members).reshape(32, 16, LANES)
    share = (jnp.sum(parts.astype(F32), axis=0) / 32.0).astype(BF16)
    mean = gathered_from(share, "member", members).reshape(8 * LEV, LANES)

    innovations = call(
        innovations_kernel, shape(SLOTS, CH, OBS), [VMEM] * 5, flops=130_000_000, traffic=2_000_000
    )(jacobian, early, late, owned, channel_mask.T)
    perturbed = call(
        perturbed_kernel, shape(SLOTS, CH, OBS, dtype=BF16), [VMEM] * 4, flops=130_000_000, traffic=1_000_000
    )(jacobian, early, late, mean)
    final_state = jnp.swapaxes(final, 0, 1)[None]
    return final_state, innovations[None], perturbed[None]


def solution(mesh):
    placed = (
        P("member", None, "tile", None),
        P(None, "tile", None),
        P(None, "tile", None),
        P(),
        P("tile", None, None),
        P(),
        P(None, "tile"),
        P(),
        P(),
        P("member", None, None, "tile"),
    )
    return jax.shard_map(
        local,
        mesh=mesh,
        in_specs=placed,
        out_specs=(
            P("member", None, "tile", None),
            P("member", None, None, "tile"),
            P("member", None, None, "tile"),
        ),
        check_vma=False,
    )
```

```python
import jax
import jax.numpy as jnp
import numpy as np
from jax import lax
from jax.experimental import pallas as pl
from jax.experimental.pallas import tpu as pltpu
from jax.sharding import PartitionSpec as P

F32 = jnp.float32
BF16 = jnp.bfloat16
SLOTS = 4
LEV = 64
NX = 1280
WIDE = 20
LANES = 128
TILES = NX // LANES
OBS = 256
CH = 256
VMEM = pl.BlockSpec(memory_space=pltpu.VMEM)
SMEM = pl.BlockSpec(memory_space=pltpu.SMEM)
ANY = pl.BlockSpec(memory_space=pl.ANY)


def split(value):
    high = value.astype(BF16)
    return high, (value - high.astype(F32)).astype(BF16)


def stacked(value):
    high, low = split(value)
    return jnp.concatenate([high, high, low, low], axis=0)


def vertical(matrices, even, odd, rows, store):
    width = len(rows) * LANES
    lane = lax.broadcasted_iota(jnp.int32, (LEV, width), 1) % LANES
    for tile in range(TILES):
        cut = slice(tile * LANES, (tile + 1) * LANES)
        upper = jnp.concatenate([even[row, :, cut] for row in rows], axis=1)
        lower = jnp.concatenate([odd[row, :, cut] for row in rows], axis=1)
        right = jnp.concatenate([upper, upper, lower, lower], axis=0)
        first = tile * LANES // (2 * WIDE)
        last = (tile * LANES + LANES - 1) // (2 * WIDE)
        mixed = jnp.dot(
            matrices[first * LEV : (last + 1) * LEV, :], right, preferred_element_type=F32
        )
        out = mixed[:LEV]
        for pair in range(first + 1, last + 1):
            at = (pair - first) * LEV
            out = jnp.where(lane >= pair * 2 * WIDE - tile * LANES, mixed[at : at + LEV], out)
        for place, row in enumerate(rows):
            store(row, cut, out[:, place * LANES : (place + 1) * LANES])


def pick(read, cells, out_ref, at):
    total = jnp.zeros((2 * LEV, OBS), F32)
    steps = NX // 256
    for chunk in range(2 * steps):
        row, start = chunk // steps, (chunk % steps) * 256
        left = jnp.concatenate(split(read(row, slice(start, start + 256))), axis=0)
        cell = lax.broadcasted_iota(jnp.int32, (256, OBS), 0) + chunk * 256
        chosen = jnp.where(cell == cells, 1.0, 0.0).astype(BF16)
        total = total + jnp.dot(left, chosen, preferred_element_type=F32)
    value = total[:LEV] + total[LEV:]
    out_ref[at : at + LEV, :] = value[:, :LANES]
    out_ref[at + LEV : at + 2 * LEV, :] = value[:, LANES:]


def fetch(sem, target, source, far=None, over=None):
    if far is None:
        pltpu.make_async_copy(source, target, sem).start()
    else:

        @pl.when(jnp.logical_not(far))
        def _():
            pltpu.make_async_copy(source, target, sem).start()

        @pl.when(far)
        def _():
            pltpu.make_async_copy(over, target, sem).start()

    return pltpu.make_async_copy(source, target, sem)


def fetch_matrices(here, near, other_core, matrices, sems):
    blocks = []
    for core in range(2):
        piece = near if core == 0 else other_core
        for y in range(4):
            for z in range(2):
                tile = jnp.bitwise_xor(here & 9, 8 * z + core) + 2 * y
                at = pl.multiple_of(tile * LANES, LANES)
                blocks.append(
                    fetch(
                        sems.at[len(blocks)],
                        matrices.at[pl.ds(at, LANES), :],
                        piece.at[y, pl.ds(z * LANES, LANES), :],
                    )
                )
    return blocks


def fetch_numbers(here, numbers, own, south, north, beyond, sems):
    two = pl.ds(2, 2)
    first = pl.ds(0, 2)
    return [
        fetch(sems.at[0], numbers.at[0], south.at[two], here == 8, beyond.at[two]),
        fetch(sems.at[1], numbers.at[1], own.at[first]),
        fetch(sems.at[2], numbers.at[2], own.at[pl.ds(4, 2)]),
        fetch(sems.at[3], numbers.at[3], north.at[first], here == 7, beyond.at[first]),
    ]


def column_of(row_ref):
    diagonal = lax.broadcasted_iota(jnp.int32, (LEV, LEV), 0) == lax.broadcasted_iota(jnp.int32, (LEV, LEV), 1)
    return jnp.sum(jnp.where(diagonal, row_ref[...], 0.0), axis=1, keepdims=True)


def two_slots(here, line, numbers, spread, evens, matrices, blocks, parts, state, even, odd, stored, first_done):
    centre_part, east_part, north_part = parts
    for row in range(4):
        cross = numbers[row, 0].astype(F32) + spread
        along = numbers[row, 1].astype(F32) + spread
        east_part[row] = cross
        north_part[row] = along
        centre_part[row] = 1.0 - 2.0 * spread - cross - along
    for slot in range(2):
        count = 4 - 2 * slot
        for row in range(count):
            at = slot + row
            if slot == 0:
                low, mid, high = line(row), line(row + 1), line(row + 2)
            else:
                low, mid, high = state[row], state[row + 1], state[row + 2]
            west = pltpu.roll(mid, 1, 1)
            east = pltpu.roll(mid, NX - 1, 1)
            value = (
                centre_part[at] * mid
                + east_part[at] * west
                + north_part[at] * low
                + spread * (east + high)
            )
            if count == 4 and row == 0:
                value = value * jnp.where(here == 0, 0.0, 1.0)
            if count == 4 and row == 3:
                value = value * jnp.where(here == 15, 0.0, 1.0)
            value = value.astype(BF16)
            masked = value * evens
            even[row] = masked
            odd[row] = value - masked
        if slot == 0:
            for block in blocks:
                block.wait()

            def keep(row, cut, value):
                state[row, :, cut] = value

            vertical(matrices, even, odd, range(4), keep)
            first_done()
        else:
            vertical(matrices, even, odd, range(2), stored)


def first_kernel(
    place, own, south, north, beyond, near, far, spread_ref, evens,
    states_out, halo_out,
    rows, numbers, matrices, centre_part, east_part, north_part, state, later, even, odd, sems,
):
    here = place[0]
    two = pl.ds(2, 2)
    first = pl.ds(0, 2)
    loads = [
        fetch(sems.at[0], rows.at[first], south.at[first], here == 8, beyond.at[first]),
        fetch(sems.at[1], rows.at[two], own.at[two]),
        fetch(sems.at[2], rows.at[pl.ds(4, 2)], north.at[two], here == 7, beyond.at[two]),
    ]
    loads += fetch_numbers(here, numbers, own, south, north, beyond, sems.at[pl.ds(3, 4)])
    blocks = fetch_matrices(here, near, far, matrices, sems.at[pl.ds(7, 16)])
    for load in loads:
        load.wait()
    stores = [
        pltpu.make_async_copy(state.at[pl.ds(1, 2)], states_out.at[first], sems.at[0]),
        pltpu.make_async_copy(later, states_out.at[two], sems.at[1]),
    ]

    def stored(row, cut, value):
        later[row, :, cut] = value
        halo_out[row, :, cut] = value.astype(BF16)

    two_slots(
        here, lambda row: rows[row].astype(F32), numbers, column_of(spread_ref), jnp.concatenate([evens[...]] * 4, axis=0), matrices, blocks,
        (centre_part, east_part, north_part), state, even, odd, stored, stores[0].start,
    )
    stores[1].start()
    for store in stores:
        store.wait()


def second_kernel(
    place, own, south, north, beyond, near, far, spread_ref, evens,
    states, south_mid, north_mid, beyond_mid, cells,
    final_out, picked_out,
    mid, sides, numbers, matrices, centre_part, east_part, north_part, state, even, odd, sems,
):
    here = place[0]
    first = pl.ds(0, 2)
    loads = [
        fetch(sems.at[0], mid, states.at[pl.ds(2, 2)]),
        fetch(sems.at[1], sides.at[first], south_mid, here == 8, beyond_mid),
        fetch(sems.at[2], sides.at[pl.ds(2, 2)], north_mid, here == 7, beyond_mid),
    ]
    loads += fetch_numbers(here, numbers, own, south, north, beyond, sems.at[pl.ds(3, 4)])
    blocks = fetch_matrices(here, near, far, matrices, sems.at[pl.ds(7, 16)])
    for load in loads:
        load.wait()

    def line(row):
        if 2 <= row < 4:
            return mid[row - 2]
        return sides[row if row < 2 else row - 2].astype(F32)

    def first_done():
        pick(lambda row, cut: state[row + 1, :, cut], cells[2:3, :], picked_out, 0)

    def stored(row, cut, value):
        mid[row, :, cut] = value
        final_out[row, :, cut] = value.astype(BF16)

    two_slots(
        here, line, numbers, column_of(spread_ref), jnp.concatenate([evens[...]] * 4, axis=0), matrices, blocks,
        (centre_part, east_part, north_part), state, even, odd, stored, first_done,
    )
    pick(lambda row, cut: mid[row, :, cut], cells[3:4, :], picked_out, 2 * LEV)


def early_kernel(states, cells, picked_out):
    pick(lambda row, cut: states[row, :, cut], cells[0:1, :], picked_out, 0)
    pick(lambda row, cut: states[row + 2, :, cut], cells[1:2, :], picked_out, 2 * LEV)


def operator(jacobian_ref):
    high, low = split(jacobian_ref[...])
    return jnp.concatenate([high, low, high, low], axis=1)


def innovations_kernel(jacobian_ref, early, late, owned, mask, out_ref):
    left = operator(jacobian_ref)
    for slot in range(SLOTS):
        picked = early if slot < 2 else late
        at = slot % 2 * 2 * LEV
        right = jnp.concatenate([picked[at : at + LEV, :], picked[at + LEV : at + 2 * LEV, :]], axis=1)
        modeled = jnp.dot(left, stacked(right), preferred_element_type=F32)
        used = mask[:, slot : slot + 1] == 1
        out_ref[slot] = jnp.where(used, owned[slot].astype(F32) - modeled, 0.0)


def perturbed_kernel(jacobian_ref, early, late, mean, out_ref):
    left = operator(jacobian_ref)
    for slot in range(SLOTS):
        picked = early if slot < 2 else late
        at = slot % 2 * 2 * LEV
        whole = slot * 2 * LEV
        right = jnp.concatenate(
            [
                picked[at + half : at + half + LEV, :] - mean[whole + half : whole + half + LEV, :].astype(F32)
                for half in (0, LEV)
            ],
            axis=1,
        )
        out_ref[slot] = jnp.dot(left, stacked(right), preferred_element_type=F32).astype(BF16)


def call(kernel, out_shape, in_specs, scratch=(), flops=0, traffic=0, limit=16 * 1024 * 1024, out_specs=None):
    return pl.pallas_call(
        kernel,
        out_shape=out_shape,
        in_specs=in_specs,
        out_specs=jax.tree.map(lambda _: VMEM, out_shape) if out_specs is None else out_specs,
        scratch_shapes=list(scratch),
        compiler_params=pltpu.CompilerParams(vmem_limit_bytes=limit),
        cost_estimate=pl.CostEstimate(flops=flops, bytes_accessed=traffic, transcendentals=0),
    )


def shape(*sizes, dtype=F32):
    return jax.ShapeDtypeStruct(sizes, dtype)


def share_kernel(parts, out_ref):
    total = parts[0].astype(F32)
    for member in range(1, 32):
        total = total + parts[member].astype(F32)
    share = (total * (1.0 / 32.0)).astype(BF16)
    for member in range(32):
        out_ref[member] = share


def gathered_from(value, axis, groups):
    count = len(groups[0])
    copies = jnp.broadcast_to(value[None], (count, *value.shape))
    return lax.all_to_all(copies, axis, 0, 0, tiled=True, axis_index_groups=groups)


AXES = ("member", "tile")
Z_GROUPS = [[4 * z + x for z in range(8)] for x in range(4)]
X_GROUPS = [[4 * z + x for x in range(4)] for z in range(8)]


def device(z, x, y, core):
    return ((z % 8) * 4 + x) * 16 + (z // 8 % 2) * 8 + y * 2 + core


def over_the_gap():
    apart, across = [], []
    for z in range(8):
        for x in range(4):
            column, back = z % 4, 1 if z >= 4 else 0
            low, high = device(z, x, 3, 1), device(z + 8, x, 0, 0)
            up, down = device(z - back, x, column, 0), device(z + 8 - back, x, column, 1)
            apart += [(low, up), (high, down)]
            across += [(up, high), (down, low)]
    return apart, across


def local(
    increment,
    courant_x,
    courant_y,
    diffusivity,
    column_inverse,
    jacobian,
    obs_cells,
    owner,
    channel_mask,
    departures,
):
    here = lax.axis_index("tile")
    member = lax.axis_index("member")
    place = jnp.reshape(here, (1,)).astype(jnp.int32)

    inverse = column_inverse.reshape(2, 2, LEV, LEV)
    upper = lax.reduce_precision(inverse, exponent_bits=8, mantissa_bits=7)
    halves = jnp.concatenate([upper.astype(BF16), (inverse - upper).astype(BF16)], axis=3)
    halves = jnp.concatenate([halves[:, 0], halves[:, 1]], axis=2).reshape(2 * LEV, 4 * LEV)
    mirrored = [
        (device(z, x, y, core), device(15 - z, x, y, core))
        for z in range(16)
        for x in range(4)
        for y in range(4)
        for core in range(2)
    ]
    other = lax.ppermute(halves, AXES, mirrored)
    increment, courant_x, courant_y, _ = lax.optimization_barrier((increment, courant_x, courant_y, halves))
    rows_in = jnp.swapaxes(increment[0], 0, 1)
    x_rows = jnp.swapaxes(courant_x, 0, 1)
    y_rows = jnp.swapaxes(courant_y, 0, 1)
    own = jnp.concatenate([x_rows[:1], y_rows[:1], rows_in, x_rows[1:], y_rows[1:]], axis=0)
    apart, across = over_the_gap()
    halfway = lax.ppermute(lax.dynamic_slice_in_dim(own, jnp.where(here == 8, 0, 2), 4), AXES, apart)
    departures, _ = lax.optimization_barrier((departures, own))
    slot_owner = lax.dynamic_index_in_dim(owner, member % 4, keepdims=False)
    offered = lax.all_to_all(departures[0], "member", 0, 0, tiled=True, axis_index_groups=X_GROUPS)
    halfway, other, offered, own = lax.optimization_barrier((halfway, other, offered, own))

    beyond = lax.ppermute(halfway, AXES, across)
    pair = jnp.concatenate([halves, other], axis=0)
    y_groups = [[8 * z + 2 * y + core for y in range(4)] for z in range(2) for core in range(2)]
    near = gathered_from(pair, "tile", y_groups).reshape(4, 4 * LEV, 4 * LEV)
    chosen = lax.dynamic_index_in_dim(offered, slot_owner % 4, keepdims=False)
    chosen, _ = lax.optimization_barrier((chosen, near))
    pieces = lax.all_to_all(chosen.reshape(8, 32, OBS), "member", 0, 0, tiled=True, axis_index_groups=Z_GROUPS)
    forward = [(i, i + 1) for i in range(15) if i != 7]
    backward = [(i + 1, i) for i in range(15) if i != 7]
    south = lax.ppermute(own[2:], "tile", forward)
    north = lax.ppermute(own[:4], "tile", backward)
    far = lax.ppermute(near, "tile", [(i, i ^ 1) for i in range(16)])

    cells = obs_cells - here * (2 * NX)
    spread = diffusivity.reshape(1, LEV)
    evens = np.broadcast_to((np.arange(NX) // WIDE % 2 == 0), (16, NX)).astype(BF16)
    fields = [own, south, north, beyond, near, far]
    window = [
        pltpu.VMEM((4, 2, LEV, NX), BF16),
        pltpu.VMEM((32 * LEV, 4 * LEV), BF16),
        pltpu.VMEM((4, LEV, NX), F32),
        pltpu.VMEM((4, LEV, NX), F32),
        pltpu.VMEM((4, LEV, NX), F32),
        pltpu.VMEM((4, LEV, NX), F32),
    ]
    masks = [
        pltpu.VMEM((4, LEV, NX), BF16),
        pltpu.VMEM((4, LEV, NX), BF16),
        pltpu.SemaphoreType.DMA((23,)),
    ]
    states, halo = call(
        first_kernel,
        (shape(4, LEV, NX), shape(2, LEV, NX, dtype=BF16)),
        [SMEM] + [ANY] * 6 + [VMEM] * 2,
        [pltpu.VMEM((6, LEV, NX), BF16), *window, pltpu.VMEM((2, LEV, NX), F32), *masks],
        flops=2_000_000_000,
        limit=56 * 1024 * 1024,
        out_specs=(ANY, VMEM),
    )(place, *fields, spread, evens)

    halfway_mid = lax.ppermute(halo, AXES, apart)
    pieces, halfway_mid = lax.optimization_barrier((pieces, halfway_mid))
    kept = lax.dynamic_index_in_dim(pieces, slot_owner // 4, keepdims=False)
    south_mid = lax.ppermute(halo, "tile", forward)
    north_mid = lax.ppermute(halo, "tile", backward)
    beyond_mid = lax.ppermute(halfway_mid, AXES, across)
    early = call(early_kernel, shape(4 * LEV, LANES), [VMEM] * 2, flops=200_000_000, traffic=2_000_000)(states, cells)
    whole = gathered_from(kept, "member", Z_GROUPS).reshape(CH, OBS)
    whole, beyond_mid = lax.optimization_barrier((whole, beyond_mid))
    owned = gathered_from(whole, "member", X_GROUPS).reshape(SLOTS, CH, OBS)
    final, late = call(
        second_kernel,
        (shape(2, LEV, NX, dtype=BF16), shape(4 * LEV, LANES)),
        [SMEM] + [ANY] * 6 + [VMEM] * 2 + [ANY] * 4 + [VMEM],
        [pltpu.VMEM((2, LEV, NX), F32), pltpu.VMEM((4, LEV, NX), BF16), *window, *masks],
        flops=2_000_000_000,
        traffic=8_000_000,
        limit=56 * 1024 * 1024,
    )(place, *fields, spread, evens, states, south_mid, north_mid, beyond_mid, cells)

    both = jnp.concatenate([early, late], axis=0).astype(BF16).reshape(32, 16, LANES)
    both, owned = lax.optimization_barrier((both, owned))
    members = [list(range(32))]
    parts = lax.all_to_all(both, "member", 0, 0, tiled=True, axis_index_groups=members).reshape(32, 16, LANES)
    shares = call(share_kernel, shape(32, 16, LANES, dtype=BF16), [VMEM], flops=70_000, traffic=300_000)(parts)
    mean = lax.all_to_all(shares, "member", 0, 0, tiled=True, axis_index_groups=members).reshape(8 * LEV, LANES)
    innovations = call(
        innovations_kernel, shape(SLOTS, CH, OBS), [VMEM] * 5, flops=130_000_000, traffic=2_000_000
    )(jacobian, early, late, owned, channel_mask.T)
    perturbed = call(
        perturbed_kernel, shape(SLOTS, CH, OBS, dtype=BF16), [VMEM] * 4, flops=130_000_000, traffic=1_000_000
    )(jacobian, early, late, mean)
    final_state = jnp.swapaxes(final, 0, 1)[None]
    return final_state, innovations[None], perturbed[None]


def solution(mesh):
    placed = (
        P("member", None, "tile", None),
        P(None, "tile", None),
        P(None, "tile", None),
        P(),
        P("tile", None, None),
        P(),
        P(None, "tile"),
        P(),
        P(),
        P("member", None, None, "tile"),
    )
    return jax.shard_map(
        local,
        mesh=mesh,
        in_specs=placed,
        out_specs=(
            P("member", None, "tile", None),
            P("member", None, None, "tile"),
            P("member", None, None, "tile"),
        ),
        check_vma=False,
    )
```

```python
import jax
import jax.numpy as jnp
import numpy as np
from jax import lax
from jax.experimental import pallas as pl
from jax.experimental.pallas import tpu as pltpu
from jax.sharding import PartitionSpec as P

F32 = jnp.float32
BF16 = jnp.bfloat16
SLOTS = 4
LEV = 64
NX = 1280
WIDE = 20
LANES = 128
TILES = NX // LANES
OBS = 256
CH = 256
VMEM = pl.BlockSpec(memory_space=pltpu.VMEM)
SMEM = pl.BlockSpec(memory_space=pltpu.SMEM)
ANY = pl.BlockSpec(memory_space=pl.ANY)


def split(value):
    high = value.astype(BF16)
    return high, (value - high.astype(F32)).astype(BF16)


def stacked(value):
    high, low = split(value)
    return jnp.concatenate([high, high, low, low], axis=0)


def vertical(matrices, even, odd, rows, store):
    width = len(rows) * LANES
    lane = lax.broadcasted_iota(jnp.int32, (LEV, width), 1) % LANES
    for tile in range(TILES):
        cut = slice(tile * LANES, (tile + 1) * LANES)
        upper = jnp.concatenate([even[row, :, cut] for row in rows], axis=1)
        lower = jnp.concatenate([odd[row, :, cut] for row in rows], axis=1)
        right = jnp.concatenate([upper, upper, lower, lower], axis=0)
        first = tile * LANES // (2 * WIDE)
        last = (tile * LANES + LANES - 1) // (2 * WIDE)
        mixed = jnp.dot(
            matrices[first * LEV : (last + 1) * LEV, :], right, preferred_element_type=F32
        )
        out = mixed[:LEV]
        for pair in range(first + 1, last + 1):
            at = (pair - first) * LEV
            out = jnp.where(lane >= pair * 2 * WIDE - tile * LANES, mixed[at : at + LEV], out)
        for place, row in enumerate(rows):
            store(row, cut, out[:, place * LANES : (place + 1) * LANES])


def pick(read, cells, out_ref, at):
    total = jnp.zeros((2 * LEV, OBS), F32)
    steps = NX // 256
    for chunk in range(2 * steps):
        row, start = chunk // steps, (chunk % steps) * 256
        left = jnp.concatenate(split(read(row, slice(start, start + 256))), axis=0)
        cell = lax.broadcasted_iota(jnp.int32, (256, OBS), 0) + chunk * 256
        chosen = jnp.where(cell == cells, 1.0, 0.0).astype(BF16)
        total = total + jnp.dot(left, chosen, preferred_element_type=F32)
    value = total[:LEV] + total[LEV:]
    out_ref[at : at + LEV, :] = value[:, :LANES]
    out_ref[at + LEV : at + 2 * LEV, :] = value[:, LANES:]


def fetch(sem, target, source, far=None, over=None):
    if far is None:
        pltpu.make_async_copy(source, target, sem).start()
    else:

        @pl.when(jnp.logical_not(far))
        def _():
            pltpu.make_async_copy(source, target, sem).start()

        @pl.when(far)
        def _():
            pltpu.make_async_copy(over, target, sem).start()

    return pltpu.make_async_copy(source, target, sem)


def fetch_matrices(here, near, other_core, matrices, sems):
    blocks = []
    for core in range(2):
        piece = near if core == 0 else other_core
        for y in range(4):
            for z in range(2):
                tile = jnp.bitwise_xor(here & 9, 8 * z + core) + 2 * y
                at = pl.multiple_of(tile * LANES, LANES)
                blocks.append(
                    fetch(
                        sems.at[len(blocks)],
                        matrices.at[pl.ds(at, LANES), :],
                        piece.at[y, pl.ds(z * LANES, LANES), :],
                    )
                )
    return blocks


def fetch_numbers(here, numbers, own, south, north, beyond, sems):
    two = pl.ds(2, 2)
    first = pl.ds(0, 2)
    return [
        fetch(sems.at[0], numbers.at[0], south.at[two], here == 8, beyond.at[two]),
        fetch(sems.at[1], numbers.at[1], own.at[first]),
        fetch(sems.at[2], numbers.at[2], own.at[pl.ds(4, 2)]),
        fetch(sems.at[3], numbers.at[3], north.at[first], here == 7, beyond.at[first]),
    ]


def column_of(row_ref):
    diagonal = lax.broadcasted_iota(jnp.int32, (LEV, LEV), 0) == lax.broadcasted_iota(jnp.int32, (LEV, LEV), 1)
    return jnp.sum(jnp.where(diagonal, row_ref[...], 0.0), axis=1, keepdims=True)


def two_slots(here, line, numbers, spread, evens, matrices, blocks, parts, state, even, odd, stored, first_done):
    centre_part, east_part, north_part = parts
    for row in range(4):
        cross = numbers[row, 0].astype(F32) + spread
        along = numbers[row, 1].astype(F32) + spread
        east_part[row] = cross
        north_part[row] = along
        centre_part[row] = 1.0 - 2.0 * spread - cross - along
    for slot in range(2):
        count = 4 - 2 * slot
        for row in range(count):
            at = slot + row
            if slot == 0:
                low, mid, high = line(row), line(row + 1), line(row + 2)
            else:
                low, mid, high = state[row], state[row + 1], state[row + 2]
            west = pltpu.roll(mid, 1, 1)
            east = pltpu.roll(mid, NX - 1, 1)
            value = (
                centre_part[at] * mid
                + east_part[at] * west
                + north_part[at] * low
                + spread * (east + high)
            )
            if count == 4 and row == 0:
                value = value * jnp.where(here == 0, 0.0, 1.0)
            if count == 4 and row == 3:
                value = value * jnp.where(here == 15, 0.0, 1.0)
            value = value.astype(BF16)
            masked = value * evens
            even[row] = masked
            odd[row] = value - masked
        if slot == 0:
            for block in blocks:
                block.wait()

            def keep(row, cut, value):
                state[row, :, cut] = value

            vertical(matrices, even, odd, range(4), keep)
            first_done()
        else:
            vertical(matrices, even, odd, range(2), stored)


def first_kernel(
    place, own, south, north, beyond, near, far, spread_ref, evens,
    states_out, halo_out,
    rows, numbers, matrices, centre_part, east_part, north_part, state, later, even, odd, sems,
):
    here = place[0]
    two = pl.ds(2, 2)
    first = pl.ds(0, 2)
    loads = [
        fetch(sems.at[0], rows.at[first], south.at[first], here == 8, beyond.at[first]),
        fetch(sems.at[1], rows.at[two], own.at[two]),
        fetch(sems.at[2], rows.at[pl.ds(4, 2)], north.at[two], here == 7, beyond.at[two]),
    ]
    loads += fetch_numbers(here, numbers, own, south, north, beyond, sems.at[pl.ds(3, 4)])
    blocks = fetch_matrices(here, near, far, matrices, sems.at[pl.ds(7, 16)])
    for load in loads:
        load.wait()
    stores = [
        pltpu.make_async_copy(state.at[pl.ds(1, 2)], states_out.at[first], sems.at[0]),
        pltpu.make_async_copy(later, states_out.at[two], sems.at[1]),
    ]

    def stored(row, cut, value):
        later[row, :, cut] = value
        halo_out[row, :, cut] = value.astype(BF16)

    two_slots(
        here, lambda row: rows[row].astype(F32), numbers, column_of(spread_ref), jnp.concatenate([evens[...]] * 4, axis=0), matrices, blocks,
        (centre_part, east_part, north_part), state, even, odd, stored, stores[0].start,
    )
    stores[1].start()
    for store in stores:
        store.wait()


def second_kernel(
    place, own, south, north, beyond, near, far, spread_ref, evens,
    states, south_mid, north_mid, beyond_mid, cells,
    final_out, picked_out,
    mid, sides, numbers, matrices, centre_part, east_part, north_part, state, even, odd, sems,
):
    here = place[0]
    first = pl.ds(0, 2)
    loads = [
        fetch(sems.at[0], mid, states.at[pl.ds(2, 2)]),
        fetch(sems.at[1], sides.at[first], south_mid, here == 8, beyond_mid),
        fetch(sems.at[2], sides.at[pl.ds(2, 2)], north_mid, here == 7, beyond_mid),
    ]
    loads += fetch_numbers(here, numbers, own, south, north, beyond, sems.at[pl.ds(3, 4)])
    blocks = fetch_matrices(here, near, far, matrices, sems.at[pl.ds(7, 16)])
    for load in loads:
        load.wait()

    def line(row):
        if 2 <= row < 4:
            return mid[row - 2]
        return sides[row if row < 2 else row - 2].astype(F32)

    def first_done():
        pick(lambda row, cut: state[row + 1, :, cut], cells[2:3, :], picked_out, 0)

    def stored(row, cut, value):
        mid[row, :, cut] = value
        final_out[row, :, cut] = value.astype(BF16)

    two_slots(
        here, line, numbers, column_of(spread_ref), jnp.concatenate([evens[...]] * 4, axis=0), matrices, blocks,
        (centre_part, east_part, north_part), state, even, odd, stored, first_done,
    )
    pick(lambda row, cut: mid[row, :, cut], cells[3:4, :], picked_out, 2 * LEV)


def early_kernel(states, cells, picked_out):
    pick(lambda row, cut: states[row, :, cut], cells[0:1, :], picked_out, 0)
    pick(lambda row, cut: states[row + 2, :, cut], cells[1:2, :], picked_out, 2 * LEV)


def operator(jacobian_ref):
    high, low = split(jacobian_ref[...])
    return jnp.concatenate([high, low, high, low], axis=1)


def innovations_kernel(jacobian_ref, early, late, owned, mask, out_ref):
    left = operator(jacobian_ref)
    for slot in range(SLOTS):
        picked = early if slot < 2 else late
        at = slot % 2 * 2 * LEV
        right = jnp.concatenate([picked[at : at + LEV, :], picked[at + LEV : at + 2 * LEV, :]], axis=1)
        modeled = jnp.dot(left, stacked(right), preferred_element_type=F32)
        used = mask[:, slot : slot + 1] == 1
        out_ref[slot] = jnp.where(used, owned[slot].astype(F32) - modeled, 0.0)


def perturbed_kernel(jacobian_ref, early, late, mean, out_ref):
    left = operator(jacobian_ref)
    for slot in range(SLOTS):
        picked = early if slot < 2 else late
        at = slot % 2 * 2 * LEV
        whole = slot * 2 * LEV
        right = jnp.concatenate(
            [
                picked[at + half : at + half + LEV, :] - mean[whole + half : whole + half + LEV, :].astype(F32)
                for half in (0, LEV)
            ],
            axis=1,
        )
        out_ref[slot] = jnp.dot(left, stacked(right), preferred_element_type=F32).astype(BF16)


def call(kernel, out_shape, in_specs, scratch=(), flops=0, traffic=0, limit=16 * 1024 * 1024, out_specs=None):
    return pl.pallas_call(
        kernel,
        out_shape=out_shape,
        in_specs=in_specs,
        out_specs=jax.tree.map(lambda _: VMEM, out_shape) if out_specs is None else out_specs,
        scratch_shapes=list(scratch),
        compiler_params=pltpu.CompilerParams(vmem_limit_bytes=limit),
        cost_estimate=pl.CostEstimate(flops=flops, bytes_accessed=traffic, transcendentals=0),
    )


def shape(*sizes, dtype=F32):
    return jax.ShapeDtypeStruct(sizes, dtype)


def share_kernel(parts, out_ref):
    total = parts[0].astype(F32)
    for member in range(1, 32):
        total = total + parts[member].astype(F32)
    share = (total * (1.0 / 32.0)).astype(BF16)
    for member in range(32):
        out_ref[member] = share


def gathered_from(value, axis, groups):
    count = len(groups[0])
    copies = jnp.broadcast_to(value[None], (count, *value.shape))
    return lax.all_to_all(copies, axis, 0, 0, tiled=True, axis_index_groups=groups)


AXES = ("member", "tile")
X_GROUPS = [[4 * z + x for x in range(4)] for z in range(8)]


def device(z, x, y, core):
    return ((z % 8) * 4 + x) * 16 + (z // 8 % 2) * 8 + y * 2 + core


def over_the_gap():
    apart, across = [], []
    for z in range(8):
        for x in range(4):
            column, back = z % 4, 1 if z >= 4 else 0
            low, high = device(z, x, 3, 1), device(z + 8, x, 0, 0)
            up, down = device(z - back, x, column, 0), device(z + 8 - back, x, column, 1)
            apart += [(low, up), (high, down)]
            across += [(up, high), (down, low)]
    return apart, across


def spread_along_z(value, offset, distance):
    arrived = lax.ppermute(value, "member", [(i, i ^ (4 * distance)) for i in range(32)])
    return jnp.where(offset & distance != 0, arrived, value)


def local(
    increment,
    courant_x,
    courant_y,
    diffusivity,
    column_inverse,
    jacobian,
    obs_cells,
    owner,
    channel_mask,
    departures,
):
    here = lax.axis_index("tile")
    member = lax.axis_index("member")
    place = jnp.reshape(here, (1,)).astype(jnp.int32)

    inverse = column_inverse.reshape(2, 2, LEV, LEV)
    upper = lax.reduce_precision(inverse, exponent_bits=8, mantissa_bits=7)
    halves = jnp.concatenate([upper.astype(BF16), (inverse - upper).astype(BF16)], axis=3)
    halves = jnp.concatenate([halves[:, 0], halves[:, 1]], axis=2).reshape(2 * LEV, 4 * LEV)
    mirrored = [
        (device(z, x, y, core), device(15 - z, x, y, core))
        for z in range(16)
        for x in range(4)
        for y in range(4)
        for core in range(2)
    ]
    other = lax.ppermute(halves, AXES, mirrored)
    increment, courant_x, courant_y, _ = lax.optimization_barrier((increment, courant_x, courant_y, halves))
    rows_in = jnp.swapaxes(increment[0], 0, 1)
    x_rows = jnp.swapaxes(courant_x, 0, 1)
    y_rows = jnp.swapaxes(courant_y, 0, 1)
    own = jnp.concatenate([x_rows[:1], y_rows[:1], rows_in, x_rows[1:], y_rows[1:]], axis=0)
    apart, across = over_the_gap()
    halfway = lax.ppermute(lax.dynamic_slice_in_dim(own, jnp.where(here == 8, 0, 2), 4), AXES, apart)
    departures, _ = lax.optimization_barrier((departures, own))
    slot_owner = lax.dynamic_index_in_dim(owner, member % 4, keepdims=False)
    offset = jnp.bitwise_xor(slot_owner // 4, member // 4)
    offered = lax.all_to_all(departures[0], "member", 0, 0, tiled=True, axis_index_groups=X_GROUPS)
    halfway, other, offered, own = lax.optimization_barrier((halfway, other, offered, own))

    beyond = lax.ppermute(halfway, AXES, across)
    pair = jnp.concatenate([halves, other], axis=0)
    y_groups = [[8 * z + 2 * y + core for y in range(4)] for z in range(2) for core in range(2)]
    near = gathered_from(pair, "tile", y_groups).reshape(4, 4 * LEV, 4 * LEV)
    chosen = lax.dynamic_index_in_dim(offered, slot_owner % 4, keepdims=False)
    chosen = spread_along_z(chosen, offset, 1)
    forward = [(i, i + 1) for i in range(15) if i != 7]
    backward = [(i + 1, i) for i in range(15) if i != 7]
    own, near, chosen = lax.optimization_barrier((own, near, chosen))
    chosen = spread_along_z(chosen, offset, 2)
    chosen, place = lax.optimization_barrier((chosen, place))
    whole = spread_along_z(chosen, offset, 4)
    south = lax.ppermute(own[2:], "tile", forward)
    north = lax.ppermute(own[:4], "tile", backward)
    far = lax.ppermute(near, "tile", [(i, i ^ 1) for i in range(16)])

    cells = obs_cells - here * (2 * NX)
    spread = diffusivity.reshape(1, LEV)
    evens = np.broadcast_to((np.arange(NX) // WIDE % 2 == 0), (16, NX)).astype(BF16)
    fields = [own, south, north, beyond, near, far]
    window = [
        pltpu.VMEM((4, 2, LEV, NX), BF16),
        pltpu.VMEM((32 * LEV, 4 * LEV), BF16),
        pltpu.VMEM((4, LEV, NX), F32),
        pltpu.VMEM((4, LEV, NX), F32),
        pltpu.VMEM((4, LEV, NX), F32),
        pltpu.VMEM((4, LEV, NX), F32),
    ]
    masks = [
        pltpu.VMEM((4, LEV, NX), BF16),
        pltpu.VMEM((4, LEV, NX), BF16),
        pltpu.SemaphoreType.DMA((23,)),
    ]
    states, halo = call(
        first_kernel,
        (shape(4, LEV, NX), shape(2, LEV, NX, dtype=BF16)),
        [SMEM] + [ANY] * 6 + [VMEM] * 2,
        [pltpu.VMEM((6, LEV, NX), BF16), *window, pltpu.VMEM((2, LEV, NX), F32), *masks],
        flops=2_000_000_000,
        limit=56 * 1024 * 1024,
        out_specs=(ANY, VMEM),
    )(place, *fields, spread, evens)

    halfway_mid = lax.ppermute(halo, AXES, apart)
    south_mid = lax.ppermute(halo, "tile", forward)
    north_mid = lax.ppermute(halo, "tile", backward)
    beyond_mid = lax.ppermute(halfway_mid, AXES, across)
    early = call(early_kernel, shape(4 * LEV, LANES), [VMEM] * 2, flops=200_000_000, traffic=2_000_000)(states, cells)
    owned = gathered_from(whole, "member", X_GROUPS).reshape(SLOTS, CH, OBS)
    final, late = call(
        second_kernel,
        (shape(2, LEV, NX, dtype=BF16), shape(4 * LEV, LANES)),
        [SMEM] + [ANY] * 6 + [VMEM] * 2 + [ANY] * 4 + [VMEM],
        [pltpu.VMEM((2, LEV, NX), F32), pltpu.VMEM((4, LEV, NX), BF16), *window, *masks],
        flops=2_000_000_000,
        traffic=8_000_000,
        limit=56 * 1024 * 1024,
    )(place, *fields, spread, evens, states, south_mid, north_mid, beyond_mid, cells)

    both = jnp.concatenate([early, late], axis=0).astype(BF16).reshape(32, 16, LANES)
    both, owned = lax.optimization_barrier((both, owned))
    members = [list(range(32))]
    parts = lax.all_to_all(both, "member", 0, 0, tiled=True, axis_index_groups=members).reshape(32, 16, LANES)
    shares = call(share_kernel, shape(32, 16, LANES, dtype=BF16), [VMEM], flops=70_000, traffic=300_000)(parts)
    mean = lax.all_to_all(shares, "member", 0, 0, tiled=True, axis_index_groups=members).reshape(8 * LEV, LANES)
    innovations = call(
        innovations_kernel, shape(SLOTS, CH, OBS), [VMEM] * 5, flops=130_000_000, traffic=2_000_000
    )(jacobian, early, late, owned, channel_mask.T)
    perturbed = call(
        perturbed_kernel, shape(SLOTS, CH, OBS, dtype=BF16), [VMEM] * 4, flops=130_000_000, traffic=1_000_000
    )(jacobian, early, late, mean)
    final_state = jnp.swapaxes(final, 0, 1)[None]
    return final_state, innovations[None], perturbed[None]


def solution(mesh):
    placed = (
        P("member", None, "tile", None),
        P(None, "tile", None),
        P(None, "tile", None),
        P(),
        P("tile", None, None),
        P(),
        P(None, "tile"),
        P(),
        P(),
        P("member", None, None, "tile"),
    )
    return jax.shard_map(
        local,
        mesh=mesh,
        in_specs=placed,
        out_specs=(
            P("member", None, "tile", None),
            P("member", None, None, "tile"),
            P("member", None, None, "tile"),
        ),
        check_vma=False,
    )
```

```python
import jax
import jax.numpy as jnp
from jax import lax
from jax.experimental import pallas as pl
from jax.experimental.pallas import tpu as pltpu
from jax.sharding import PartitionSpec as P

F32 = jnp.float32
BF16 = jnp.bfloat16
SLOTS = 4
LEV = 64
NX = 1280
WIDE = 20
LANES = 128
TILES = NX // LANES
OBS = 256
CH = 256
VMEM = pl.BlockSpec(memory_space=pltpu.VMEM)
SMEM = pl.BlockSpec(memory_space=pltpu.SMEM)
ANY = pl.BlockSpec(memory_space=pl.ANY)


def split(value):
    high = value.astype(BF16)
    return high, (value - high.astype(F32)).astype(BF16)


def stacked(value):
    high, low = split(value)
    return jnp.concatenate([high, high, low, low], axis=0)


def vertical(matrices, even, odd, rows, store):
    width = len(rows) * LANES
    lane = lax.broadcasted_iota(jnp.int32, (LEV, width), 1) % LANES
    for tile in range(TILES):
        cut = slice(tile * LANES, (tile + 1) * LANES)
        upper = jnp.concatenate([even[row, :, cut] for row in rows], axis=1)
        lower = jnp.concatenate([odd[row, :, cut] for row in rows], axis=1)
        right = jnp.concatenate([upper, upper, lower, lower], axis=0)
        first = tile * LANES // (2 * WIDE)
        last = (tile * LANES + LANES - 1) // (2 * WIDE)
        mixed = jnp.dot(
            matrices[first * LEV : (last + 1) * LEV, :], right, preferred_element_type=F32
        )
        out = mixed[:LEV]
        for pair in range(first + 1, last + 1):
            at = (pair - first) * LEV
            out = jnp.where(lane >= pair * 2 * WIDE - tile * LANES, mixed[at : at + LEV], out)
        for place, row in enumerate(rows):
            store(row, cut, out[:, place * LANES : (place + 1) * LANES])


def pick(read, cells, out_ref, at):
    total = jnp.zeros((2 * LEV, OBS), F32)
    steps = NX // 256
    for chunk in range(2 * steps):
        row, start = chunk // steps, (chunk % steps) * 256
        left = jnp.concatenate(split(read(row, slice(start, start + 256))), axis=0)
        cell = lax.broadcasted_iota(jnp.int32, (256, OBS), 0) + chunk * 256
        chosen = jnp.where(cell == cells, 1.0, 0.0).astype(BF16)
        total = total + jnp.dot(left, chosen, preferred_element_type=F32)
    value = total[:LEV] + total[LEV:]
    out_ref[at : at + LEV, :] = value[:, :LANES]
    out_ref[at + LEV : at + 2 * LEV, :] = value[:, LANES:]


def fetch(sem, target, source, far=None, over=None):
    if far is None:
        pltpu.make_async_copy(source, target, sem).start()
    else:

        @pl.when(jnp.logical_not(far))
        def _():
            pltpu.make_async_copy(source, target, sem).start()

        @pl.when(far)
        def _():
            pltpu.make_async_copy(over, target, sem).start()

    return pltpu.make_async_copy(source, target, sem)


def fetch_matrices(here, near, other_core, matrices, sems):
    blocks = []
    for core in range(2):
        piece = near if core == 0 else other_core
        for y in range(4):
            for z in range(2):
                tile = jnp.bitwise_xor(here & 9, 8 * z + core) + 2 * y
                at = pl.multiple_of(tile * LANES, LANES)
                blocks.append(
                    fetch(
                        sems.at[len(blocks)],
                        matrices.at[pl.ds(at, LANES), :],
                        piece.at[y, pl.ds(z * LANES, LANES), :],
                    )
                )
    return blocks


def fetch_numbers(here, numbers, own, south, north, beyond, sems):
    two = pl.ds(2, 2)
    first = pl.ds(0, 2)
    return [
        fetch(sems.at[0], numbers.at[0], south.at[two], here == 8, beyond.at[two]),
        fetch(sems.at[1], numbers.at[1], own.at[first]),
        fetch(sems.at[2], numbers.at[2], own.at[pl.ds(4, 2)]),
        fetch(sems.at[3], numbers.at[3], north.at[first], here == 7, beyond.at[first]),
    ]


def column_of(row_ref):
    diagonal = lax.broadcasted_iota(jnp.int32, (LEV, LEV), 0) == lax.broadcasted_iota(jnp.int32, (LEV, LEV), 1)
    return jnp.sum(jnp.where(diagonal, row_ref[...], 0.0), axis=1, keepdims=True)


def even_blocks():
    lane = lax.broadcasted_iota(jnp.int32, (16, NX), 1)
    block = (lane * 52429) >> 20
    return jnp.concatenate([(1 - (block & 1)).astype(F32).astype(BF16)] * 4, axis=0)


def two_slots(here, line, numbers, spread, evens, matrices, waits, parts, state, even, odd, stored, first_done):
    centre_part, east_part, north_part = parts
    first_loads, loads, blocks, numbers_ready = waits
    for row in range(4):
        if row < len(first_loads):
            first_loads[row].wait()
        cross = numbers[row, 0].astype(F32) + spread
        along = numbers[row, 1].astype(F32) + spread
        east_part[row] = cross
        north_part[row] = along
        centre_part[row] = 1.0 - 2.0 * spread - cross - along
    numbers_ready()
    for load in loads:
        load.wait()
    for slot in range(2):
        count = 4 - 2 * slot
        for row in range(count):
            at = slot + row
            if slot == 0:
                low, mid, high = line(row), line(row + 1), line(row + 2)
            else:
                low, mid, high = state[row], state[row + 1], state[row + 2]
            west = pltpu.roll(mid, 1, 1)
            east = pltpu.roll(mid, NX - 1, 1)
            value = (
                centre_part[at] * mid
                + east_part[at] * west
                + north_part[at] * low
                + spread * (east + high)
            )
            if count == 4 and row == 0:
                value = value * jnp.where(here == 0, 0.0, 1.0)
            if count == 4 and row == 3:
                value = value * jnp.where(here == 15, 0.0, 1.0)
            value = value.astype(BF16)
            masked = value * evens
            even[row] = masked
            odd[row] = value - masked
        if slot == 0:
            for block in blocks:
                block.wait()

            def keep(row, cut, value):
                state[row, :, cut] = value

            vertical(matrices, even, odd, range(4), keep)
            first_done()
        else:
            vertical(matrices, even, odd, range(2), stored)


def first_kernel(
    place, own, south, north, beyond, near, far, spread_ref,
    states_out, numbers_out, halo_out,
    rows, numbers, matrices, centre_part, east_part, north_part, state, later, halo, even, odd, sems,
):
    here = place[0]
    two = pl.ds(2, 2)
    first = pl.ds(0, 2)
    first_loads = fetch_numbers(here, numbers, own, south, north, beyond, sems.at[pl.ds(3, 4)])
    loads = [
        fetch(sems.at[0], rows.at[first], south.at[first], here == 8, beyond.at[first]),
        fetch(sems.at[1], rows.at[two], own.at[two]),
        fetch(sems.at[2], rows.at[pl.ds(4, 2)], north.at[two], here == 7, beyond.at[two]),
    ]
    blocks = fetch_matrices(here, near, far, matrices, sems.at[pl.ds(7, 16)])
    stores = [
        pltpu.make_async_copy(state.at[pl.ds(1, 2)], states_out.at[first], sems.at[23]),
        pltpu.make_async_copy(later, states_out.at[two], sems.at[24]),
        pltpu.make_async_copy(numbers, numbers_out, sems.at[25]),
        pltpu.make_async_copy(halo, halo_out, sems.at[26]),
    ]

    def stored(row, cut, value):
        later[row, :, cut] = value
        halo[row, :, cut] = value.astype(BF16)

    two_slots(
        here, lambda row: rows[row].astype(F32), numbers, column_of(spread_ref), even_blocks(), matrices,
        (first_loads, loads, blocks, stores[2].start), (centre_part, east_part, north_part), state, even, odd, stored,
        stores[0].start,
    )
    stores[3].start()
    stores[1].start()
    for store in stores:
        store.wait()


def second_kernel(
    place, numbers_in, near, far, spread_ref,
    states, south_mid, north_mid, beyond_mid, cells, early,
    final_out, picked_out, both_out,
    mid, sides, numbers, matrices, centre_part, east_part, north_part, state, even, odd, sems,
):
    here = place[0]
    first = pl.ds(0, 2)
    first_loads = [fetch(sems.at[3], numbers, numbers_in)]
    loads = [
        fetch(sems.at[0], mid, states.at[pl.ds(2, 2)]),
        fetch(sems.at[1], sides.at[first], south_mid, here == 8, beyond_mid),
        fetch(sems.at[2], sides.at[pl.ds(2, 2)], north_mid, here == 7, beyond_mid),
    ]
    blocks = fetch_matrices(here, near, far, matrices, sems.at[pl.ds(7, 16)])

    def line(row):
        if 2 <= row < 4:
            return mid[row - 2]
        return sides[row if row < 2 else row - 2].astype(F32)

    def first_done():
        pick(lambda row, cut: state[row + 1, :, cut], cells[2:3, :], picked_out, 0)

    def stored(row, cut, value):
        mid[row, :, cut] = value
        final_out[row, :, cut] = value.astype(BF16)

    two_slots(
        here, line, numbers, column_of(spread_ref), even_blocks(), matrices,
        (first_loads, loads, blocks, lambda: None), (centre_part, east_part, north_part), state, even, odd, stored,
        first_done,
    )
    pick(lambda row, cut: mid[row, :, cut], cells[3:4, :], picked_out, 2 * LEV)
    both_out[: 4 * LEV, :] = early[...].astype(BF16)
    both_out[4 * LEV :, :] = picked_out[...].astype(BF16)


def early_kernel(states, cells, picked_out):
    pick(lambda row, cut: states[row, :, cut], cells[0:1, :], picked_out, 0)
    pick(lambda row, cut: states[row + 2, :, cut], cells[1:2, :], picked_out, 2 * LEV)


def operator(jacobian_ref):
    high, low = split(jacobian_ref[...])
    return jnp.concatenate([high, low, high, low], axis=1)


def innovations_kernel(jacobian_ref, early, late, owned, mask, out_ref):
    left = operator(jacobian_ref)
    for slot in range(SLOTS):
        picked = early if slot < 2 else late
        at = slot % 2 * 2 * LEV
        right = jnp.concatenate([picked[at : at + LEV, :], picked[at + LEV : at + 2 * LEV, :]], axis=1)
        modeled = jnp.dot(left, stacked(right), preferred_element_type=F32)
        used = mask[:, slot : slot + 1] == 1
        out_ref[slot] = jnp.where(used, owned[slot].astype(F32) - modeled, 0.0)


def perturbed_kernel(jacobian_ref, early, late, mean, out_ref):
    left = operator(jacobian_ref)
    for slot in range(SLOTS):
        picked = early if slot < 2 else late
        at = slot % 2 * 2 * LEV
        whole = slot * 2 * LEV
        right = jnp.concatenate(
            [
                picked[at + half : at + half + LEV, :] - mean[whole + half : whole + half + LEV, :].astype(F32)
                for half in (0, LEV)
            ],
            axis=1,
        )
        out_ref[slot] = jnp.dot(left, stacked(right), preferred_element_type=F32).astype(BF16)


def call(kernel, out_shape, in_specs, scratch=(), flops=0, traffic=0, limit=16 * 1024 * 1024, out_specs=None):
    return pl.pallas_call(
        kernel,
        out_shape=out_shape,
        in_specs=in_specs,
        out_specs=jax.tree.map(lambda _: VMEM, out_shape) if out_specs is None else out_specs,
        scratch_shapes=list(scratch),
        compiler_params=pltpu.CompilerParams(vmem_limit_bytes=limit),
        cost_estimate=pl.CostEstimate(flops=flops, bytes_accessed=traffic, transcendentals=0),
    )


def shape(*sizes, dtype=F32):
    return jax.ShapeDtypeStruct(sizes, dtype)


def share_kernel(parts, out_ref):
    total = parts[0].astype(F32)
    for member in range(1, 32):
        total = total + parts[member].astype(F32)
    share = (total * (1.0 / 32.0)).astype(BF16)
    for member in range(32):
        out_ref[member] = share


def gathered_from(value, axis, groups):
    count = len(groups[0])
    copies = jnp.broadcast_to(value[None], (count, *value.shape))
    return lax.all_to_all(copies, axis, 0, 0, tiled=True, axis_index_groups=groups)


AXES = ("member", "tile")
X_GROUPS = [[4 * z + x for x in range(4)] for z in range(8)]


def device(z, x, y, core):
    return ((z % 8) * 4 + x) * 16 + (z // 8 % 2) * 8 + y * 2 + core


def over_the_gap():
    apart, across = [], []
    for z in range(8):
        for x in range(4):
            column, back = z % 4, 1 if z >= 4 else 0
            low, high = device(z, x, 3, 1), device(z + 8, x, 0, 0)
            up, down = device(z - back, x, column, 0), device(z + 8 - back, x, column, 1)
            apart += [(low, up), (high, down)]
            across += [(up, high), (down, low)]
    return apart, across


def spread_along_z(value, offset, distance):
    arrived = lax.ppermute(value, "member", [(i, i ^ (4 * distance)) for i in range(32)])
    return jnp.where(offset & distance != 0, arrived, value)


def local(
    increment,
    courant_x,
    courant_y,
    diffusivity,
    column_inverse,
    jacobian,
    obs_cells,
    owner,
    channel_mask,
    departures,
):
    here = lax.axis_index("tile")
    member = lax.axis_index("member")
    place = jnp.reshape(here, (1,)).astype(jnp.int32)

    inverse = column_inverse.reshape(2, 2, LEV, LEV)
    upper = lax.reduce_precision(inverse, exponent_bits=8, mantissa_bits=7)
    halves = jnp.concatenate([upper.astype(BF16), (inverse - upper).astype(BF16)], axis=3)
    halves = jnp.concatenate([halves[:, 0], halves[:, 1]], axis=2).reshape(2 * LEV, 4 * LEV)
    mirrored = [
        (device(z, x, y, core), device(15 - z, x, y, core))
        for z in range(16)
        for x in range(4)
        for y in range(4)
        for core in range(2)
    ]
    other = lax.ppermute(halves, AXES, mirrored)
    increment, courant_x, courant_y, _ = lax.optimization_barrier((increment, courant_x, courant_y, halves))
    rows_in = jnp.swapaxes(increment[0], 0, 1)
    x_rows = jnp.swapaxes(courant_x, 0, 1)
    y_rows = jnp.swapaxes(courant_y, 0, 1)
    own = jnp.concatenate([x_rows[:1], y_rows[:1], rows_in, x_rows[1:], y_rows[1:]], axis=0)
    apart, across = over_the_gap()
    halfway = lax.ppermute(lax.dynamic_slice_in_dim(own, jnp.where(here == 8, 0, 2), 4), AXES, apart)
    departures, _ = lax.optimization_barrier((departures, own))
    slot_owner = lax.dynamic_index_in_dim(owner, member % 4, keepdims=False)
    offset = jnp.bitwise_xor(slot_owner // 4, member // 4)
    offered = lax.all_to_all(departures[0], "member", 0, 0, tiled=True, axis_index_groups=X_GROUPS)
    halfway, other, offered, own = lax.optimization_barrier((halfway, other, offered, own))

    beyond = lax.ppermute(halfway, AXES, across)
    pair = jnp.concatenate([halves, other], axis=0)
    y_groups = [[8 * z + 2 * y + core for y in range(4)] for z in range(2) for core in range(2)]
    near = gathered_from(pair, "tile", y_groups).reshape(4, 4 * LEV, 4 * LEV)
    chosen = lax.dynamic_index_in_dim(offered, slot_owner % 4, keepdims=False)
    chosen = spread_along_z(chosen, offset, 1)
    forward = [(i, i + 1) for i in range(15) if i != 7]
    backward = [(i + 1, i) for i in range(15) if i != 7]
    own, near, chosen = lax.optimization_barrier((own, near, chosen))
    chosen = spread_along_z(chosen, offset, 2)
    chosen, place = lax.optimization_barrier((chosen, place))
    whole = spread_along_z(chosen, offset, 4)
    south = lax.ppermute(own[2:], "tile", forward)
    north = lax.ppermute(own[:4], "tile", backward)
    far = lax.ppermute(near, "tile", [(i, i ^ 1) for i in range(16)])

    cells = obs_cells - here * (2 * NX)
    spread = diffusivity.reshape(1, LEV)
    fields = [own, south, north, beyond, near, far]
    window = [
        pltpu.VMEM((4, 2, LEV, NX), BF16),
        pltpu.VMEM((32 * LEV, 4 * LEV), BF16),
        pltpu.VMEM((4, LEV, NX), F32),
        pltpu.VMEM((4, LEV, NX), F32),
        pltpu.VMEM((4, LEV, NX), F32),
        pltpu.VMEM((4, LEV, NX), F32),
    ]
    masks = [
        pltpu.VMEM((4, LEV, NX), BF16),
        pltpu.VMEM((4, LEV, NX), BF16),
        pltpu.SemaphoreType.DMA((27,)),
    ]
    states, numbers, halo = call(
        first_kernel,
        (shape(4, LEV, NX), shape(4, 2, LEV, NX, dtype=BF16), shape(2, LEV, NX, dtype=BF16)),
        [SMEM] + [ANY] * 6 + [VMEM],
        [pltpu.VMEM((6, LEV, NX), BF16), *window, pltpu.VMEM((2, LEV, NX), F32), pltpu.VMEM((2, LEV, NX), BF16), *masks],
        flops=2_000_000_000,
        limit=56 * 1024 * 1024,
        out_specs=(ANY, ANY, ANY),
    )(place, *fields, spread)

    halfway_mid = lax.ppermute(halo, AXES, apart)
    south_mid = lax.ppermute(halo, "tile", forward)
    north_mid = lax.ppermute(halo, "tile", backward)
    beyond_mid = lax.ppermute(halfway_mid, AXES, across)
    early = call(early_kernel, shape(4 * LEV, LANES), [VMEM] * 2, flops=200_000_000, traffic=2_000_000)(states, cells)
    owned = gathered_from(whole, "member", X_GROUPS).reshape(SLOTS, CH, OBS)
    final, late, both = call(
        second_kernel,
        (shape(2, LEV, NX, dtype=BF16), shape(4 * LEV, LANES), shape(8 * LEV, LANES, dtype=BF16)),
        [SMEM] + [ANY] * 3 + [VMEM] + [ANY] * 4 + [VMEM] * 2,
        [pltpu.VMEM((2, LEV, NX), F32), pltpu.VMEM((4, LEV, NX), BF16), *window, *masks],
        flops=2_000_000_000,
        traffic=8_000_000,
        limit=56 * 1024 * 1024,
    )(place, numbers, near, far, spread, states, south_mid, north_mid, beyond_mid, cells, early)

    both = both.reshape(32, 16, LANES)
    both, owned = lax.optimization_barrier((both, owned))
    members = [list(range(32))]
    parts = lax.all_to_all(both, "member", 0, 0, tiled=True, axis_index_groups=members).reshape(32, 16, LANES)
    shares = call(share_kernel, shape(32, 16, LANES, dtype=BF16), [VMEM], flops=70_000, traffic=300_000)(parts)
    mean = lax.all_to_all(shares, "member", 0, 0, tiled=True, axis_index_groups=members).reshape(8 * LEV, LANES)
    innovations = call(
        innovations_kernel, shape(SLOTS, CH, OBS), [VMEM] * 5, flops=130_000_000, traffic=2_000_000
    )(jacobian, early, late, owned, channel_mask.T)
    perturbed = call(
        perturbed_kernel, shape(SLOTS, CH, OBS, dtype=BF16), [VMEM] * 4, flops=130_000_000, traffic=1_000_000
    )(jacobian, early, late, mean)
    final_state = jnp.swapaxes(final, 0, 1)[None]
    return final_state, innovations[None], perturbed[None]


def solution(mesh):
    placed = (
        P("member", None, "tile", None),
        P(None, "tile", None),
        P(None, "tile", None),
        P(),
        P("tile", None, None),
        P(),
        P(None, "tile"),
        P(),
        P(),
        P("member", None, None, "tile"),
    )
    return jax.shard_map(
        local,
        mesh=mesh,
        in_specs=placed,
        out_specs=(
            P("member", None, "tile", None),
            P("member", None, None, "tile"),
            P("member", None, None, "tile"),
        ),
        check_vma=False,
    )
```

```python
import functools

import jax
import jax.numpy as jnp
from jax import lax
from jax.experimental import pallas as pl
from jax.experimental.pallas import tpu as pltpu
from jax.sharding import PartitionSpec as P

F32 = jnp.float32
BF16 = jnp.bfloat16
SLOTS = 4
LEV = 64
NX = 1280
WIDE = 20
LANES = 128
TILES = NX // LANES
OBS = 256
CH = 256
VMEM = pl.BlockSpec(memory_space=pltpu.VMEM)
SMEM = pl.BlockSpec(memory_space=pltpu.SMEM)
ANY = pl.BlockSpec(memory_space=pl.ANY)


def split(value):
    high = value.astype(BF16)
    return high, (value - high.astype(F32)).astype(BF16)


def stacked(value):
    high, low = split(value)
    return jnp.concatenate([high, high, low, low], axis=0)


def vertical(matrices, even, odd, rows, store):
    width = len(rows) * LANES
    lane = lax.broadcasted_iota(jnp.int32, (LEV, width), 1) % LANES
    for tile in range(TILES):
        cut = slice(tile * LANES, (tile + 1) * LANES)
        upper = jnp.concatenate([even[row, :, cut] for row in rows], axis=1)
        lower = jnp.concatenate([odd[row, :, cut] for row in rows], axis=1)
        right = jnp.concatenate([upper, upper, lower, lower], axis=0)
        first = tile * LANES // (2 * WIDE)
        last = (tile * LANES + LANES - 1) // (2 * WIDE)
        mixed = jnp.dot(
            matrices[first * LEV : (last + 1) * LEV, :], right, preferred_element_type=F32
        )
        out = mixed[:LEV]
        for pair in range(first + 1, last + 1):
            at = (pair - first) * LEV
            out = jnp.where(lane >= pair * 2 * WIDE - tile * LANES, mixed[at : at + LEV], out)
        for place, row in enumerate(rows):
            store(row, cut, out[:, place * LANES : (place + 1) * LANES])


def pick(read, cells, out_ref, at):
    total = jnp.zeros((2 * LEV, OBS), F32)
    steps = NX // 256
    for chunk in range(2 * steps):
        row, start = chunk // steps, (chunk % steps) * 256
        left = jnp.concatenate(split(read(row, slice(start, start + 256))), axis=0)
        cell = lax.broadcasted_iota(jnp.int32, (256, OBS), 0) + chunk * 256
        chosen = jnp.where(cell == cells, 1.0, 0.0).astype(BF16)
        total = total + jnp.dot(left, chosen, preferred_element_type=F32)
    value = total[:LEV] + total[LEV:]
    out_ref[at : at + LEV, :] = value[:, :LANES]
    out_ref[at + LEV : at + 2 * LEV, :] = value[:, LANES:]


def fetch(sem, target, source, far=None, over=None):
    if far is None:
        pltpu.make_async_copy(source, target, sem).start()
    else:

        @pl.when(jnp.logical_not(far))
        def _():
            pltpu.make_async_copy(source, target, sem).start()

        @pl.when(far)
        def _():
            pltpu.make_async_copy(over, target, sem).start()

    return pltpu.make_async_copy(source, target, sem)


def fetch_matrices(here, near, other_core, matrices, sems):
    blocks = []
    for core in range(2):
        piece = near if core == 0 else other_core
        for y in range(4):
            for z in range(2):
                tile = jnp.bitwise_xor(here & 9, 8 * z + core) + 2 * y
                at = pl.multiple_of(tile * LANES, LANES)
                blocks.append(
                    fetch(
                        sems.at[len(blocks)],
                        matrices.at[pl.ds(at, LANES), :],
                        piece.at[y, pl.ds(z * LANES, LANES), :],
                    )
                )
    return blocks


def fetch_numbers(here, numbers, own, south, north, beyond, sems):
    two = pl.ds(2, 2)
    first = pl.ds(0, 2)
    return [
        fetch(sems.at[0], numbers.at[0], south.at[two], here == 8, beyond.at[two]),
        fetch(sems.at[1], numbers.at[1], own.at[first]),
        fetch(sems.at[2], numbers.at[2], own.at[pl.ds(4, 2)]),
        fetch(sems.at[3], numbers.at[3], north.at[first], here == 7, beyond.at[first]),
    ]


def column_of(row_ref):
    diagonal = lax.broadcasted_iota(jnp.int32, (LEV, LEV), 0) == lax.broadcasted_iota(jnp.int32, (LEV, LEV), 1)
    return jnp.sum(jnp.where(diagonal, row_ref[...], 0.0), axis=1, keepdims=True)


def even_blocks():
    lane = lax.broadcasted_iota(jnp.int32, (16, NX), 1)
    block = (lane * 52429) >> 20
    return jnp.concatenate([(1 - (block & 1)).astype(F32).astype(BF16)] * 4, axis=0)


def two_slots(here, line, numbers, spread, evens, matrices, waits, parts, state, even, odd, stored, first_done):
    centre_part, east_part, north_part = parts
    first_loads, loads, blocks, numbers_ready = waits
    for row in range(4):
        if row < len(first_loads):
            first_loads[row].wait()
        cross = numbers[row, 0].astype(F32) + spread
        along = numbers[row, 1].astype(F32) + spread
        east_part[row] = cross
        north_part[row] = along
        centre_part[row] = 1.0 - 2.0 * spread - cross - along
    numbers_ready()
    for load in loads:
        load.wait()
    for slot in range(2):
        count = 4 - 2 * slot
        for row in range(count):
            at = slot + row
            if slot == 0:
                low, mid, high = line(row), line(row + 1), line(row + 2)
            else:
                low, mid, high = state[row], state[row + 1], state[row + 2]
            west = pltpu.roll(mid, 1, 1)
            east = pltpu.roll(mid, NX - 1, 1)
            value = (
                centre_part[at] * mid
                + east_part[at] * west
                + north_part[at] * low
                + spread * (east + high)
            )
            if count == 4 and row == 0:
                value = value * jnp.where(here == 0, 0.0, 1.0)
            if count == 4 and row == 3:
                value = value * jnp.where(here == 15, 0.0, 1.0)
            value = value.astype(BF16)
            masked = value * evens
            even[row] = masked
            odd[row] = value - masked
        if slot == 0:
            for block in blocks:
                block.wait()

            def keep(row, cut, value):
                state[row, :, cut] = value

            vertical(matrices, even, odd, range(4), keep)
            first_done()
        else:
            vertical(matrices, even, odd, range(2), stored)


def first_kernel(
    place, own, south, north, beyond, near, far, spread_ref,
    states_out, numbers_out, halo_out,
    rows, numbers, matrices, centre_part, east_part, north_part, state, later, halo, even, odd, sems,
):
    here = place[0]
    two = pl.ds(2, 2)
    first = pl.ds(0, 2)
    first_loads = fetch_numbers(here, numbers, own, south, north, beyond, sems.at[pl.ds(3, 4)])
    loads = [
        fetch(sems.at[0], rows.at[first], south.at[first], here == 8, beyond.at[first]),
        fetch(sems.at[1], rows.at[two], own.at[two]),
        fetch(sems.at[2], rows.at[pl.ds(4, 2)], north.at[two], here == 7, beyond.at[two]),
    ]
    blocks = fetch_matrices(here, near, far, matrices, sems.at[pl.ds(7, 16)])
    stores = [
        pltpu.make_async_copy(state.at[pl.ds(1, 2)], states_out.at[first], sems.at[23]),
        pltpu.make_async_copy(later, states_out.at[two], sems.at[24]),
        pltpu.make_async_copy(numbers, numbers_out, sems.at[25]),
        pltpu.make_async_copy(halo, halo_out, sems.at[26]),
    ]

    def stored(row, cut, value):
        later[row, :, cut] = value
        halo[row, :, cut] = value.astype(BF16)

    two_slots(
        here, lambda row: rows[row].astype(F32), numbers, column_of(spread_ref), even_blocks(), matrices,
        (first_loads, loads, blocks, stores[2].start), (centre_part, east_part, north_part), state, even, odd, stored,
        stores[0].start,
    )
    stores[3].start()
    stores[1].start()
    for store in stores:
        store.wait()


def second_kernel(
    place, numbers_in, near, far, spread_ref,
    states, south_mid, north_mid, beyond_mid, cells, early,
    final_out, picked_out, both_out,
    mid, sides, numbers, matrices, centre_part, east_part, north_part, state, even, odd, sems,
):
    here = place[0]
    first = pl.ds(0, 2)
    first_loads = [fetch(sems.at[3], numbers, numbers_in)]
    loads = [
        fetch(sems.at[0], mid, states.at[pl.ds(2, 2)]),
        fetch(sems.at[1], sides.at[first], south_mid, here == 8, beyond_mid),
        fetch(sems.at[2], sides.at[pl.ds(2, 2)], north_mid, here == 7, beyond_mid),
    ]
    blocks = fetch_matrices(here, near, far, matrices, sems.at[pl.ds(7, 16)])

    def line(row):
        if 2 <= row < 4:
            return mid[row - 2]
        return sides[row if row < 2 else row - 2].astype(F32)

    def first_done():
        pick(lambda row, cut: state[row + 1, :, cut], cells[2:3, :], picked_out, 0)

    def stored(row, cut, value):
        mid[row, :, cut] = value
        final_out[row, :, cut] = value.astype(BF16)

    two_slots(
        here, line, numbers, column_of(spread_ref), even_blocks(), matrices,
        (first_loads, loads, blocks, lambda: None), (centre_part, east_part, north_part), state, even, odd, stored,
        first_done,
    )
    pick(lambda row, cut: mid[row, :, cut], cells[3:4, :], picked_out, 2 * LEV)
    both_out[: 4 * LEV, :] = early[...].astype(BF16)
    both_out[4 * LEV :, :] = picked_out[...].astype(BF16)


def early_kernel(states, cells, picked_out):
    pick(lambda row, cut: states[row, :, cut], cells[0:1, :], picked_out, 0)
    pick(lambda row, cut: states[row + 2, :, cut], cells[1:2, :], picked_out, 2 * LEV)


def operator(jacobian_ref):
    high, low = split(jacobian_ref[...])
    return jnp.concatenate([high, low, high, low], axis=1)


def innovations_kernel(jacobian_ref, early, late, owned, mask, out_ref):
    left = operator(jacobian_ref)
    for slot in range(SLOTS):
        picked = early if slot < 2 else late
        at = slot % 2 * 2 * LEV
        right = jnp.concatenate([picked[at : at + LEV, :], picked[at + LEV : at + 2 * LEV, :]], axis=1)
        modeled = jnp.dot(left, stacked(right), preferred_element_type=F32)
        used = mask[:, slot : slot + 1] == 1
        out_ref[slot] = jnp.where(used, owned[slot].astype(F32) - modeled, 0.0)


def perturbed_kernel(jacobian_ref, early, late, mean, out_ref):
    left = operator(jacobian_ref)
    for slot in range(SLOTS):
        picked = early if slot < 2 else late
        at = slot % 2 * 2 * LEV
        whole = slot * 2 * LEV
        right = jnp.concatenate(
            [
                picked[at + half : at + half + LEV, :] - mean[whole + half : whole + half + LEV, :].astype(F32)
                for half in (0, LEV)
            ],
            axis=1,
        )
        out_ref[slot] = jnp.dot(left, stacked(right), preferred_element_type=F32).astype(BF16)


def call(kernel, out_shape, in_specs, scratch=(), flops=0, traffic=0, limit=16 * 1024 * 1024, out_specs=None):
    return pl.pallas_call(
        kernel,
        out_shape=out_shape,
        in_specs=in_specs,
        out_specs=jax.tree.map(lambda _: VMEM, out_shape) if out_specs is None else out_specs,
        scratch_shapes=list(scratch),
        compiler_params=pltpu.CompilerParams(vmem_limit_bytes=limit),
        cost_estimate=pl.CostEstimate(flops=flops, bytes_accessed=traffic, transcendentals=0),
    )


def shape(*sizes, dtype=F32):
    return jax.ShapeDtypeStruct(sizes, dtype)


def share_kernel(scale, parts, out_ref):
    total = parts[0].astype(F32)
    for part in range(1, parts.shape[0]):
        total = total + parts[part].astype(F32)
    share = (total * scale).astype(BF16)
    for copy in range(out_ref.shape[0]):
        out_ref[copy] = share


def gathered_from(value, axis, groups):
    count = len(groups[0])
    copies = jnp.broadcast_to(value[None], (count, *value.shape))
    return lax.all_to_all(copies, axis, 0, 0, tiled=True, axis_index_groups=groups)


AXES = ("member", "tile")
X_GROUPS = [[4 * z + x for x in range(4)] for z in range(8)]


def device(z, x, y, core):
    return ((z % 8) * 4 + x) * 16 + (z // 8 % 2) * 8 + y * 2 + core


def over_the_gap():
    apart, across = [], []
    for z in range(8):
        for x in range(4):
            column, back = z % 4, 1 if z >= 4 else 0
            low, high = device(z, x, 3, 1), device(z + 8, x, 0, 0)
            up, down = device(z - back, x, column, 0), device(z + 8 - back, x, column, 1)
            apart += [(low, up), (high, down)]
            across += [(up, high), (down, low)]
    return apart, across


def spread_along_z(value, offset, distance):
    arrived = lax.ppermute(value, "member", [(i, i ^ (4 * distance)) for i in range(32)])
    return jnp.where(offset & distance != 0, arrived, value)


def local(
    increment,
    courant_x,
    courant_y,
    diffusivity,
    column_inverse,
    jacobian,
    obs_cells,
    owner,
    channel_mask,
    departures,
):
    here = lax.axis_index("tile")
    member = lax.axis_index("member")
    place = jnp.reshape(here, (1,)).astype(jnp.int32)

    inverse = column_inverse.reshape(2, 2, LEV, LEV)
    upper = lax.reduce_precision(inverse, exponent_bits=8, mantissa_bits=7)
    halves = jnp.concatenate([upper.astype(BF16), (inverse - upper).astype(BF16)], axis=3)
    halves = jnp.concatenate([halves[:, 0], halves[:, 1]], axis=2).reshape(2 * LEV, 4 * LEV)
    mirrored = [
        (device(z, x, y, core), device(15 - z, x, y, core))
        for z in range(16)
        for x in range(4)
        for y in range(4)
        for core in range(2)
    ]
    other = lax.ppermute(halves, AXES, mirrored)
    increment, courant_x, courant_y, _ = lax.optimization_barrier((increment, courant_x, courant_y, halves))
    rows_in = jnp.swapaxes(increment[0], 0, 1)
    x_rows = jnp.swapaxes(courant_x, 0, 1)
    y_rows = jnp.swapaxes(courant_y, 0, 1)
    own = jnp.concatenate([x_rows[:1], y_rows[:1], rows_in, x_rows[1:], y_rows[1:]], axis=0)
    apart, across = over_the_gap()
    halfway = lax.ppermute(lax.dynamic_slice_in_dim(own, jnp.where(here == 8, 0, 2), 4), AXES, apart)
    departures, _ = lax.optimization_barrier((departures, own))
    slot_owner = lax.dynamic_index_in_dim(owner, member % 4, keepdims=False)
    offset = jnp.bitwise_xor(slot_owner // 4, member // 4)
    offered = lax.all_to_all(departures[0], "member", 0, 0, tiled=True, axis_index_groups=X_GROUPS)
    halfway, other, offered, own = lax.optimization_barrier((halfway, other, offered, own))

    beyond = lax.ppermute(halfway, AXES, across)
    pair = jnp.concatenate([halves, other], axis=0)
    y_groups = [[8 * z + 2 * y + core for y in range(4)] for z in range(2) for core in range(2)]
    near = gathered_from(pair, "tile", y_groups).reshape(4, 4 * LEV, 4 * LEV)
    chosen = lax.dynamic_index_in_dim(offered, slot_owner % 4, keepdims=False)
    chosen = spread_along_z(chosen, offset, 1)
    forward = [(i, i + 1) for i in range(15) if i != 7]
    backward = [(i + 1, i) for i in range(15) if i != 7]
    own, near, chosen = lax.optimization_barrier((own, near, chosen))
    chosen = spread_along_z(chosen, offset, 2)
    chosen, place = lax.optimization_barrier((chosen, place))
    whole = spread_along_z(chosen, offset, 4)
    south = lax.ppermute(own[2:], "tile", forward)
    north = lax.ppermute(own[:4], "tile", backward)
    far = lax.ppermute(near, "tile", [(i, i ^ 1) for i in range(16)])

    cells = obs_cells - here * (2 * NX)
    spread = diffusivity.reshape(1, LEV)
    fields = [own, south, north, beyond, near, far]
    window = [
        pltpu.VMEM((4, 2, LEV, NX), BF16),
        pltpu.VMEM((32 * LEV, 4 * LEV), BF16),
        pltpu.VMEM((4, LEV, NX), F32),
        pltpu.VMEM((4, LEV, NX), F32),
        pltpu.VMEM((4, LEV, NX), F32),
        pltpu.VMEM((4, LEV, NX), F32),
    ]
    masks = [
        pltpu.VMEM((4, LEV, NX), BF16),
        pltpu.VMEM((4, LEV, NX), BF16),
        pltpu.SemaphoreType.DMA((27,)),
    ]
    states, numbers, halo = call(
        first_kernel,
        (shape(4, LEV, NX), shape(4, 2, LEV, NX, dtype=BF16), shape(2, LEV, NX, dtype=BF16)),
        [SMEM] + [ANY] * 6 + [VMEM],
        [pltpu.VMEM((6, LEV, NX), BF16), *window, pltpu.VMEM((2, LEV, NX), F32), pltpu.VMEM((2, LEV, NX), BF16), *masks],
        flops=2_000_000_000,
        limit=56 * 1024 * 1024,
        out_specs=(ANY, ANY, ANY),
    )(place, *fields, spread)

    halfway_mid = lax.ppermute(halo, AXES, apart)
    south_mid = lax.ppermute(halo, "tile", forward)
    north_mid = lax.ppermute(halo, "tile", backward)
    beyond_mid = lax.ppermute(halfway_mid, AXES, across)
    early = call(early_kernel, shape(4 * LEV, LANES), [VMEM] * 2, flops=200_000_000, traffic=2_000_000)(states, cells)
    owned = gathered_from(whole, "member", X_GROUPS).reshape(SLOTS, CH, OBS)
    final, late, both = call(
        second_kernel,
        (shape(2, LEV, NX, dtype=BF16), shape(4 * LEV, LANES), shape(8 * LEV, LANES, dtype=BF16)),
        [SMEM] + [ANY] * 3 + [VMEM] + [ANY] * 4 + [VMEM] * 2,
        [pltpu.VMEM((2, LEV, NX), F32), pltpu.VMEM((4, LEV, NX), BF16), *window, *masks],
        flops=2_000_000_000,
        traffic=8_000_000,
        limit=56 * 1024 * 1024,
    )(place, numbers, near, far, spread, states, south_mid, north_mid, beyond_mid, cells, early)

    eights = [list(range(8 * i, 8 * i + 8)) for i in range(4)]
    fours = [[8 * i + j for i in range(4)] for j in range(8)]
    both, owned = lax.optimization_barrier((both, owned))
    parts = lax.all_to_all(both.reshape(8, LEV, LANES), "member", 0, 0, tiled=True, axis_index_groups=eights)
    sums = call(
        functools.partial(share_kernel, 1.0), shape(4, LEV, LANES, dtype=BF16), [VMEM], flops=70_000, traffic=300_000
    )(parts)
    sums = lax.all_to_all(sums, "member", 0, 0, tiled=True, axis_index_groups=fours)
    shares = call(
        functools.partial(share_kernel, 1.0 / 32.0),
        shape(8, LEV, LANES, dtype=BF16),
        [VMEM],
        flops=70_000,
        traffic=300_000,
    )(sums)
    mean = lax.all_to_all(shares, "member", 0, 0, tiled=True, axis_index_groups=eights).reshape(8 * LEV, LANES)

    innovations = call(
        innovations_kernel, shape(SLOTS, CH, OBS), [VMEM] * 5, flops=130_000_000, traffic=2_000_000
    )(jacobian, early, late, owned, channel_mask.T)
    perturbed = call(
        perturbed_kernel, shape(SLOTS, CH, OBS, dtype=BF16), [VMEM] * 4, flops=130_000_000, traffic=1_000_000
    )(jacobian, early, late, mean)
    final_state = jnp.swapaxes(final, 0, 1)[None]
    return final_state, innovations[None], perturbed[None]


def solution(mesh):
    placed = (
        P("member", None, "tile", None),
        P(None, "tile", None),
        P(None, "tile", None),
        P(),
        P("tile", None, None),
        P(),
        P(None, "tile"),
        P(),
        P(),
        P("member", None, None, "tile"),
    )
    return jax.shard_map(
        local,
        mesh=mesh,
        in_specs=placed,
        out_specs=(
            P("member", None, "tile", None),
            P("member", None, None, "tile"),
            P("member", None, None, "tile"),
        ),
        check_vma=False,
    )
```

```python
import functools

import jax
import jax.numpy as jnp
from jax import lax
from jax.experimental import pallas as pl
from jax.experimental.pallas import tpu as pltpu
from jax.sharding import PartitionSpec as P

F32 = jnp.float32
BF16 = jnp.bfloat16
SLOTS = 4
LEV = 64
NX = 1280
WIDE = 20
LANES = 128
TILES = NX // LANES
OBS = 256
CH = 256
VMEM = pl.BlockSpec(memory_space=pltpu.VMEM)
SMEM = pl.BlockSpec(memory_space=pltpu.SMEM)
ANY = pl.BlockSpec(memory_space=pl.ANY)


def split(value):
    high = value.astype(BF16)
    return high, (value - high.astype(F32)).astype(BF16)


def stacked(value):
    high, low = split(value)
    return jnp.concatenate([high, high, low, low], axis=0)


def vertical(matrices, even, odd, rows, store):
    width = len(rows) * LANES
    lane = lax.broadcasted_iota(jnp.int32, (LEV, width), 1) % LANES
    for tile in range(TILES):
        cut = slice(tile * LANES, (tile + 1) * LANES)
        upper = jnp.concatenate([even[row, :, cut] for row in rows], axis=1)
        lower = jnp.concatenate([odd[row, :, cut] for row in rows], axis=1)
        right = jnp.concatenate([upper, upper, lower, lower], axis=0)
        first = tile * LANES // (2 * WIDE)
        last = (tile * LANES + LANES - 1) // (2 * WIDE)
        mixed = jnp.dot(
            matrices[first * LEV : (last + 1) * LEV, :], right, preferred_element_type=F32
        )
        out = mixed[:LEV]
        for pair in range(first + 1, last + 1):
            at = (pair - first) * LEV
            out = jnp.where(lane >= pair * 2 * WIDE - tile * LANES, mixed[at : at + LEV], out)
        for place, row in enumerate(rows):
            store(row, cut, out[:, place * LANES : (place + 1) * LANES])


def pick(read, cells, out_ref, at):
    total = jnp.zeros((2 * LEV, OBS), F32)
    steps = NX // 256
    for chunk in range(2 * steps):
        row, start = chunk // steps, (chunk % steps) * 256
        left = jnp.concatenate(split(read(row, slice(start, start + 256))), axis=0)
        cell = lax.broadcasted_iota(jnp.int32, (256, OBS), 0) + chunk * 256
        chosen = jnp.where(cell == cells, 1.0, 0.0).astype(BF16)
        total = total + jnp.dot(left, chosen, preferred_element_type=F32)
    value = total[:LEV] + total[LEV:]
    out_ref[at : at + LEV, :] = value[:, :LANES]
    out_ref[at + LEV : at + 2 * LEV, :] = value[:, LANES:]


def fetch(sem, target, source, far=None, over=None):
    if far is None:
        pltpu.make_async_copy(source, target, sem).start()
    else:

        @pl.when(jnp.logical_not(far))
        def _():
            pltpu.make_async_copy(source, target, sem).start()

        @pl.when(far)
        def _():
            pltpu.make_async_copy(over, target, sem).start()

    return pltpu.make_async_copy(source, target, sem)


def fetch_matrices(here, near, other_core, matrices, sems):
    blocks = []
    for core in range(2):
        piece = near if core == 0 else other_core
        for y in range(4):
            for z in range(2):
                tile = jnp.bitwise_xor(here & 9, 8 * z + core) + 2 * y
                at = pl.multiple_of(tile * LANES, LANES)
                blocks.append(
                    fetch(
                        sems.at[len(blocks)],
                        matrices.at[pl.ds(at, LANES), :],
                        piece.at[y, pl.ds(z * LANES, LANES), :],
                    )
                )
    return blocks


def fetch_numbers(here, numbers, own, south, north, beyond, sems):
    two = pl.ds(2, 2)
    first = pl.ds(0, 2)
    return [
        fetch(sems.at[0], numbers.at[0], south.at[two], here == 8, beyond.at[two]),
        fetch(sems.at[1], numbers.at[1], own.at[first]),
        fetch(sems.at[2], numbers.at[2], own.at[pl.ds(4, 2)]),
        fetch(sems.at[3], numbers.at[3], north.at[first], here == 7, beyond.at[first]),
    ]


def column_of(row_ref):
    diagonal = lax.broadcasted_iota(jnp.int32, (LEV, LEV), 0) == lax.broadcasted_iota(jnp.int32, (LEV, LEV), 1)
    return jnp.sum(jnp.where(diagonal, row_ref[...], 0.0), axis=1, keepdims=True)


def even_blocks():
    lane = lax.broadcasted_iota(jnp.int32, (16, NX), 1)
    block = (lane * 52429) >> 20
    return jnp.concatenate([(1 - (block & 1)).astype(F32).astype(BF16)] * 4, axis=0)


def two_slots(here, line, numbers, spread, evens, matrices, waits, parts, state, even, odd, stored, first_done):
    centre_part, east_part, north_part = parts
    first_loads, loads, blocks, numbers_ready = waits
    for row in range(4):
        if row < len(first_loads):
            first_loads[row].wait()
        cross = numbers[row, 0].astype(F32) + spread
        along = numbers[row, 1].astype(F32) + spread
        east_part[row] = cross
        north_part[row] = along
        centre_part[row] = 1.0 - 2.0 * spread - cross - along
    numbers_ready()
    for load in loads:
        load.wait()
    for slot in range(2):
        count = 4 - 2 * slot
        for row in range(count):
            at = slot + row
            if slot == 0:
                low, mid, high = line(row), line(row + 1), line(row + 2)
            else:
                low, mid, high = state[row], state[row + 1], state[row + 2]
            west = pltpu.roll(mid, 1, 1)
            east = pltpu.roll(mid, NX - 1, 1)
            value = (
                centre_part[at] * mid
                + east_part[at] * west
                + north_part[at] * low
                + spread * (east + high)
            )
            if count == 4 and row == 0:
                value = value * jnp.where(here == 0, 0.0, 1.0)
            if count == 4 and row == 3:
                value = value * jnp.where(here == 15, 0.0, 1.0)
            value = value.astype(BF16)
            masked = value * evens
            even[row] = masked
            odd[row] = value - masked
        if slot == 0:
            for block in blocks:
                block.wait()

            def keep(row, cut, value):
                state[row, :, cut] = value

            vertical(matrices, even, odd, range(4), keep)
            first_done()
        else:
            vertical(matrices, even, odd, range(2), stored)


def first_kernel(
    place, own, south, north, beyond, near, far, spread_ref,
    states_out, numbers_out, halo_out,
    rows, numbers, matrices, centre_part, east_part, north_part, state, later, halo, even, odd, sems,
):
    here = place[0]
    two = pl.ds(2, 2)
    first = pl.ds(0, 2)
    first_loads = fetch_numbers(here, numbers, own, south, north, beyond, sems.at[pl.ds(3, 4)])
    loads = [
        fetch(sems.at[0], rows.at[first], south.at[first], here == 8, beyond.at[first]),
        fetch(sems.at[1], rows.at[two], own.at[two]),
        fetch(sems.at[2], rows.at[pl.ds(4, 2)], north.at[two], here == 7, beyond.at[two]),
    ]
    blocks = fetch_matrices(here, near, far, matrices, sems.at[pl.ds(7, 16)])
    stores = [
        pltpu.make_async_copy(state.at[pl.ds(1, 2)], states_out.at[first], sems.at[23]),
        pltpu.make_async_copy(later, states_out.at[two], sems.at[24]),
        pltpu.make_async_copy(numbers, numbers_out, sems.at[25]),
        pltpu.make_async_copy(halo, halo_out, sems.at[26]),
    ]

    def stored(row, cut, value):
        later[row, :, cut] = value
        halo[row, :, cut] = value.astype(BF16)

    two_slots(
        here, lambda row: rows[row].astype(F32), numbers, column_of(spread_ref), even_blocks(), matrices,
        (first_loads, loads, blocks, stores[2].start), (centre_part, east_part, north_part), state, even, odd, stored,
        stores[0].start,
    )
    stores[3].start()
    stores[1].start()
    for store in stores:
        store.wait()


def second_kernel(
    place, numbers_in, near, far, spread_ref,
    states, south_mid, north_mid, beyond_mid, cells, early,
    final_out, picked_out, both_out,
    mid, sides, numbers, matrices, centre_part, east_part, north_part, state, even, odd, sems,
):
    here = place[0]
    first = pl.ds(0, 2)
    first_loads = [fetch(sems.at[3], numbers, numbers_in)]
    loads = [
        fetch(sems.at[0], mid, states.at[pl.ds(2, 2)]),
        fetch(sems.at[1], sides.at[first], south_mid, here == 8, beyond_mid),
        fetch(sems.at[2], sides.at[pl.ds(2, 2)], north_mid, here == 7, beyond_mid),
    ]
    blocks = fetch_matrices(here, near, far, matrices, sems.at[pl.ds(7, 16)])

    def line(row):
        if 2 <= row < 4:
            return mid[row - 2]
        return sides[row if row < 2 else row - 2].astype(F32)

    def first_done():
        pick(lambda row, cut: state[row + 1, :, cut], cells[2:3, :], picked_out, 0)

    def stored(row, cut, value):
        mid[row, :, cut] = value
        final_out[row, :, cut] = value.astype(BF16)

    two_slots(
        here, line, numbers, column_of(spread_ref), even_blocks(), matrices,
        (first_loads, loads, blocks, lambda: None), (centre_part, east_part, north_part), state, even, odd, stored,
        first_done,
    )
    pick(lambda row, cut: mid[row, :, cut], cells[3:4, :], picked_out, 2 * LEV)
    both_out[: 4 * LEV, :] = early[...].astype(BF16)
    both_out[4 * LEV :, :] = picked_out[...].astype(BF16)


def early_kernel(states, cells, picked_out):
    pick(lambda row, cut: states[row, :, cut], cells[0:1, :], picked_out, 0)
    pick(lambda row, cut: states[row + 2, :, cut], cells[1:2, :], picked_out, 2 * LEV)


def operator(jacobian_ref):
    high, low = split(jacobian_ref[...])
    return jnp.concatenate([high, low, high, low], axis=1)


def innovations_kernel(jacobian_ref, early, late, owned, mask, out_ref):
    left = operator(jacobian_ref)
    for slot in range(SLOTS):
        picked = early if slot < 2 else late
        at = slot % 2 * 2 * LEV
        right = jnp.concatenate([picked[at : at + LEV, :], picked[at + LEV : at + 2 * LEV, :]], axis=1)
        modeled = jnp.dot(left, stacked(right), preferred_element_type=F32)
        used = mask[:, slot : slot + 1] == 1
        out_ref[slot] = jnp.where(used, owned[slot].astype(F32) - modeled, 0.0)


def perturbed_kernel(jacobian_ref, early, late, mean, out_ref):
    left = operator(jacobian_ref)
    for slot in range(SLOTS):
        picked = early if slot < 2 else late
        at = slot % 2 * 2 * LEV
        whole = slot * 2 * LEV
        right = jnp.concatenate(
            [
                picked[at + half : at + half + LEV, :] - mean[whole + half : whole + half + LEV, :].astype(F32)
                for half in (0, LEV)
            ],
            axis=1,
        )
        out_ref[slot] = jnp.dot(left, stacked(right), preferred_element_type=F32).astype(BF16)


def call(kernel, out_shape, in_specs, scratch=(), flops=0, traffic=0, limit=16 * 1024 * 1024, out_specs=None):
    return pl.pallas_call(
        kernel,
        out_shape=out_shape,
        in_specs=in_specs,
        out_specs=jax.tree.map(lambda _: VMEM, out_shape) if out_specs is None else out_specs,
        scratch_shapes=list(scratch),
        compiler_params=pltpu.CompilerParams(vmem_limit_bytes=limit),
        cost_estimate=pl.CostEstimate(flops=flops, bytes_accessed=traffic, transcendentals=0),
    )


def shape(*sizes, dtype=F32):
    return jax.ShapeDtypeStruct(sizes, dtype)


def share_kernel(scale, parts, out_ref):
    total = parts[0].astype(F32)
    for part in range(1, parts.shape[0]):
        total = total + parts[part].astype(F32)
    share = (total * scale).astype(BF16)
    for copy in range(out_ref.shape[0]):
        out_ref[copy] = share


def gathered_from(value, axis, groups):
    count = len(groups[0])
    copies = jnp.broadcast_to(value[None], (count, *value.shape))
    return lax.all_to_all(copies, axis, 0, 0, tiled=True, axis_index_groups=groups)


AXES = ("member", "tile")
X_GROUPS = [[4 * z + x for x in range(4)] for z in range(8)]


def device(z, x, y, core):
    return ((z % 8) * 4 + x) * 16 + (z // 8 % 2) * 8 + y * 2 + core


def over_the_gap():
    apart, across = [], []
    for z in range(8):
        for x in range(4):
            column, back = z % 4, 1 if z >= 4 else 0
            low, high = device(z, x, 3, 1), device(z + 8, x, 0, 0)
            up, down = device(z - back, x, column, 0), device(z + 8 - back, x, column, 1)
            apart += [(low, up), (high, down)]
            across += [(up, high), (down, low)]
    return apart, across


def spread_along_z(value, offset, distance):
    arrived = lax.ppermute(value, "member", [(i, i ^ (4 * distance)) for i in range(32)])
    return jnp.where(offset & distance != 0, arrived, value)


def local(
    increment,
    courant_x,
    courant_y,
    diffusivity,
    column_inverse,
    jacobian,
    obs_cells,
    owner,
    channel_mask,
    departures,
):
    here = lax.axis_index("tile")
    member = lax.axis_index("member")
    place = jnp.reshape(here, (1,)).astype(jnp.int32)

    inverse = column_inverse.reshape(2, 2, LEV, LEV)
    upper = lax.reduce_precision(inverse, exponent_bits=8, mantissa_bits=7)
    halves = jnp.concatenate([upper.astype(BF16), (inverse - upper).astype(BF16)], axis=3)
    halves = jnp.concatenate([halves[:, 0], halves[:, 1]], axis=2).reshape(2 * LEV, 4 * LEV)
    mirrored = [
        (device(z, x, y, core), device(15 - z, x, y, core))
        for z in range(16)
        for x in range(4)
        for y in range(4)
        for core in range(2)
    ]
    other = lax.ppermute(halves, AXES, mirrored)
    increment, courant_x, courant_y, _ = lax.optimization_barrier((increment, courant_x, courant_y, halves))
    rows_in = jnp.swapaxes(increment[0], 0, 1)
    x_rows = jnp.swapaxes(courant_x, 0, 1)
    y_rows = jnp.swapaxes(courant_y, 0, 1)
    own = jnp.concatenate([x_rows[:1], y_rows[:1], rows_in, x_rows[1:], y_rows[1:]], axis=0)
    apart, across = over_the_gap()
    halfway = lax.ppermute(lax.dynamic_slice_in_dim(own, jnp.where(here == 8, 0, 2), 4), AXES, apart)
    departures, _ = lax.optimization_barrier((departures, own))
    slot_owner = lax.dynamic_index_in_dim(owner, member % 4, keepdims=False)
    offset = jnp.bitwise_xor(slot_owner // 4, member // 4)
    offered = lax.all_to_all(departures[0], "member", 0, 0, tiled=True, axis_index_groups=X_GROUPS)
    halfway, other, offered, own = lax.optimization_barrier((halfway, other, offered, own))

    beyond = lax.ppermute(halfway, AXES, across)
    pair = jnp.concatenate([halves, other], axis=0)
    y_groups = [[8 * z + 2 * y + core for y in range(4)] for z in range(2) for core in range(2)]
    near = gathered_from(pair, "tile", y_groups).reshape(4, 4 * LEV, 4 * LEV)
    chosen = lax.dynamic_index_in_dim(offered, slot_owner % 4, keepdims=False)
    chosen = spread_along_z(chosen, offset, 1)
    forward = [(i, i + 1) for i in range(15) if i != 7]
    backward = [(i + 1, i) for i in range(15) if i != 7]
    own, near, chosen = lax.optimization_barrier((own, near, chosen))
    chosen = spread_along_z(chosen, offset, 2)
    chosen, place = lax.optimization_barrier((chosen, place))
    whole = spread_along_z(chosen, offset, 4)
    south = lax.ppermute(own[2:], "tile", forward)
    north = lax.ppermute(own[:4], "tile", backward)
    far = lax.ppermute(near, "tile", [(i, i ^ 1) for i in range(16)])

    cells = obs_cells - here * (2 * NX)
    spread = diffusivity.reshape(1, LEV)
    fields = [own, south, north, beyond, near, far]
    window = [
        pltpu.VMEM((4, 2, LEV, NX), BF16),
        pltpu.VMEM((32 * LEV, 4 * LEV), BF16),
        pltpu.VMEM((4, LEV, NX), F32),
        pltpu.VMEM((4, LEV, NX), F32),
        pltpu.VMEM((4, LEV, NX), F32),
        pltpu.VMEM((4, LEV, NX), F32),
    ]
    masks = [
        pltpu.VMEM((4, LEV, NX), BF16),
        pltpu.VMEM((4, LEV, NX), BF16),
        pltpu.SemaphoreType.DMA((27,)),
    ]
    states, numbers, halo = call(
        first_kernel,
        (shape(4, LEV, NX), shape(4, 2, LEV, NX, dtype=BF16), shape(2, LEV, NX, dtype=BF16)),
        [SMEM] + [ANY] * 6 + [VMEM],
        [pltpu.VMEM((6, LEV, NX), BF16), *window, pltpu.VMEM((2, LEV, NX), F32), pltpu.VMEM((2, LEV, NX), BF16), *masks],
        flops=2_000_000_000,
        limit=50 * 1024 * 1024,
        out_specs=(ANY, ANY, ANY),
    )(place, *fields, spread)

    halfway_mid = lax.ppermute(halo, AXES, apart)
    south_mid = lax.ppermute(halo, "tile", forward)
    north_mid = lax.ppermute(halo, "tile", backward)
    beyond_mid = lax.ppermute(halfway_mid, AXES, across)
    early = call(early_kernel, shape(4 * LEV, LANES), [VMEM] * 2, flops=200_000_000, traffic=2_000_000)(states, cells)
    owned = gathered_from(whole, "member", X_GROUPS).reshape(SLOTS, CH, OBS)
    final, late, both = call(
        second_kernel,
        (shape(2, LEV, NX, dtype=BF16), shape(4 * LEV, LANES), shape(8 * LEV, LANES, dtype=BF16)),
        [SMEM] + [ANY] * 3 + [VMEM] + [ANY] * 4 + [VMEM] * 2,
        [pltpu.VMEM((2, LEV, NX), F32), pltpu.VMEM((4, LEV, NX), BF16), *window, *masks],
        flops=2_000_000_000,
        traffic=8_000_000,
        limit=50 * 1024 * 1024,
    )(place, numbers, near, far, spread, states, south_mid, north_mid, beyond_mid, cells, early)

    eights = [list(range(8 * i, 8 * i + 8)) for i in range(4)]
    fours = [[8 * i + j for i in range(4)] for j in range(8)]
    both, owned = lax.optimization_barrier((both, owned))
    parts = lax.all_to_all(both.reshape(8, LEV, LANES), "member", 0, 0, tiled=True, axis_index_groups=eights)
    sums = call(
        functools.partial(share_kernel, 1.0), shape(4, LEV, LANES, dtype=BF16), [VMEM], flops=70_000, traffic=300_000
    )(parts)
    sums = lax.all_to_all(sums, "member", 0, 0, tiled=True, axis_index_groups=fours)
    shares = call(
        functools.partial(share_kernel, 1.0 / 32.0),
        shape(8, LEV, LANES, dtype=BF16),
        [VMEM],
        flops=70_000,
        traffic=300_000,
    )(sums)
    mean = lax.all_to_all(shares, "member", 0, 0, tiled=True, axis_index_groups=eights).reshape(8 * LEV, LANES)

    innovations = call(
        innovations_kernel, shape(SLOTS, CH, OBS), [VMEM] * 5, flops=130_000_000, traffic=2_000_000
    )(jacobian, early, late, owned, channel_mask.T)
    perturbed = call(
        perturbed_kernel, shape(SLOTS, CH, OBS, dtype=BF16), [VMEM] * 4, flops=130_000_000, traffic=1_000_000
    )(jacobian, early, late, mean)
    final_state = jnp.swapaxes(final, 0, 1)[None]
    return final_state, innovations[None], perturbed[None]


def solution(mesh):
    placed = (
        P("member", None, "tile", None),
        P(None, "tile", None),
        P(None, "tile", None),
        P(),
        P("tile", None, None),
        P(),
        P(None, "tile"),
        P(),
        P(),
        P("member", None, None, "tile"),
    )
    return jax.shard_map(
        local,
        mesh=mesh,
        in_specs=placed,
        out_specs=(
            P("member", None, "tile", None),
            P("member", None, None, "tile"),
            P("member", None, None, "tile"),
        ),
        check_vma=False,
    )
```
